32 devices in a mesh: dp: 8 (over z, x), shard: 4 (over y, core).
Axes of the slice: x: 2, y: 2, z: 4, core: 2. Of those that a mesh axis runs over, the one named last changes fastest.
Arguments:
- inputs: bfloat16 [128, 256, 512], P(('dp', 'shard')), may hold values from -6 to 6
- lengths: int32 [128], P(('dp', 'shard')), may hold values from 1 to 250, as said below
- slot_order: int32 [128, 256], P(('dp', 'shard')), may hold values from 0 to 255, each once within a row
- ln1_gain: bfloat16 [512], P(('dp', 'shard')), may hold values from 0.099609375 to 1.8984375
- ln1_bias: bfloat16 [512], P(('dp', 'shard')), may hold values from -1.75 to 1.75
- w_qkv: bfloat16 [512, 1536], P(('dp', 'shard')), may hold values from -0.25 to 0.25
- q_bias: bfloat16 [512], P(('dp', 'shard')), may hold values from -1.75 to 1.75
- v_bias: bfloat16 [512], P(('dp', 'shard')), may hold values from -1.75 to 1.75
- w_out: bfloat16 [512, 512], P(('dp', 'shard')), may hold values from -2 to 2
- out_bias: bfloat16 [512], P(('dp', 'shard')), may hold values from -1.75 to 1.75
- ln2_gain: bfloat16 [512], P(('dp', 'shard')), may hold values from 0.099609375 to 1.8984375
- ln2_bias: bfloat16 [512], P(('dp', 'shard')), may hold values from -1.75 to 1.75
- w_up: bfloat16 [512, 2048], P(('dp', 'shard')), may hold values from -0.25 to 0.25
- up_bias: bfloat16 [2048], P(('dp', 'shard')), may hold values from -1.75 to 1.75
- w_down: bfloat16 [2048, 512], P(('dp', 'shard')), may hold values from -0.125 to 0.125
- down_bias: bfloat16 [512], P(('dp', 'shard')), may hold values from -1.75 to 1.75
- cotangent: bfloat16 [128, 256, 512], P(('dp', 'shard')), may hold values from -6 to 6
Outputs:
- output: bfloat16 [128, 256, 512], P(('dp', 'shard'))
- input_grad: float32 [128, 256, 512], P(('dp', 'shard'))
- ln1_gain_grad: float32 [512], P(('dp', 'shard'))
- ln1_bias_grad: float32 [512], P(('dp', 'shard'))
- w_qkv_grad: float32 [512, 1536], P(('dp', 'shard'))
- q_bias_grad: float32 [512], P(('dp', 'shard'))
- v_bias_grad: float32 [512], P(('dp', 'shard'))
- w_out_grad: float32 [512, 512], P(('dp', 'shard'))
- out_bias_grad: float32 [512], P(('dp', 'shard'))
- ln2_gain_grad: float32 [512], P(('dp', 'shard'))
- ln2_bias_grad: float32 [512], P(('dp', 'shard'))
- w_up_grad: float32 [512, 2048], P(('dp', 'shard'))
- up_bias_grad: float32 [2048], P(('dp', 'shard'))
- w_down_grad: float32 [2048, 512], P(('dp', 'shard'))
- down_bias_grad: float32 [512], P(('dp', 'shard'))
The draws below stay inside these ranges and needn't reach their ends.
Inputs may be any that keep to these rules, and one draw needn't show every extreme that they name: `lengths`: some row has exactly 250 valid slots and some row exactly 1. `slot_order`: each row is an ordering of its 256 slots.
All inputs are finite; a program needn't handle non-finite values.
Results may differ from the reference program's by a relative error of at most 0.012.
Values may be sent and summed in bfloat16 or wider, within the bound.
A program may use at most 128 MiB of HBM per device.

```python
import jax
import jax.numpy as jnp
from jax import lax

D = 512
HEADS = 8
HEAD_DIM = 64
FF = 2048
SLOTS = 256
SEQ = 250
ROWS = 128


def draw_lengths(key, part):
    key = jax.random.fold_in(key, 7)
    first_key, second_key = jax.random.split(key)
    drawn = jax.random.randint(first_key, (ROWS,), 1, SEQ + 1)
    chosen = jax.random.permutation(second_key, ROWS)
    drawn = drawn.at[chosen[0]].set(SEQ)
    drawn = drawn.at[chosen[1]].set(1)
    return drawn.astype(jnp.int32)


def with_spikes(entries, rng, source, target, blocks, factor):
    def block_of(axis_at):
        return (jnp.arange(entries.shape[axis_at]) // (entries.shape[axis_at] // blocks)).reshape((-1,) + (1,) * (entries.ndim - 1 - axis_at))

    near = jax.random.permutation(rng, blocks)[block_of(target)]
    far = (block_of(target) + blocks // 2) % blocks
    return jnp.where((block_of(source) == near) | (block_of(source) == far), factor * entries, entries)


def shard_levels(rng, shape, cuts, low, top_value):
    loudness = 1.0
    for dim, shards_of in cuts:
        heights = jax.random.uniform(jax.random.fold_in(jax.random.fold_in(rng, 6), dim), (shards_of,), jnp.float32, low / len(cuts), top_value / len(cuts))
        loudness = loudness * jnp.repeat(jnp.exp(heights), shape[dim] // shards_of).reshape((-1,) + (1,) * (len(shape) - 1 - dim))
    return loudness


def gaussian(key, shape, deviation, reach, shards=(), kind=jnp.bfloat16):
    values = deviation * jax.random.normal(key, shape, jnp.float32)
    if shards:
        values = values * shard_levels(key, shape, shards, -0.22, 0.18)
    return jnp.clip(values, -reach, reach).astype(kind)


def bell_draw_with(stream_key, shape, width, limit, shards, heavy, kind=jnp.bfloat16):
    array = width * jax.random.normal(stream_key, shape, jnp.float32)
    if shards:
        array = array * shard_levels(stream_key, shape, shards, -0.22, 0.18)
    return jnp.clip(with_spikes(array, jax.random.fold_in(stream_key, 3), *heavy), -limit, limit).astype(kind)


def setup_inputs(seed: int = 0) -> dict:
    streams_of = jax.random.split(jax.random.key(seed), 18)
    inputs = bell_draw_with(streams_of[0], (ROWS, SLOTS, D), 1.0, 6.0, ((0, 32),), (0, 2, 32, 2.75))
    lengths = draw_lengths(jax.random.fold_in(streams_of[17], 71), 0)
    slot_order = jax.vmap(lambda own: jax.random.permutation(own, SLOTS))(jax.random.split(streams_of[2], ROWS)).reshape((ROWS, SLOTS)).astype(jnp.int32)
    ln1_gain = jnp.clip(1.0 + 0.18 * jax.random.normal(streams_of[3], (D,), jnp.float32), 0.099609375, 1.8984375).astype(jnp.bfloat16)
    ln1_bias = gaussian(streams_of[4], (D,), 0.3, 1.75, ((0, 32),))
    w_qkv = gaussian(streams_of[5], (D, 3 * D), D ** -0.5, 0.25, ((0, 32),))
    q_bias = gaussian(streams_of[6], (D,), 0.3, 1.75, ((0, 32),))
    v_bias = gaussian(streams_of[7], (D,), 0.3, 1.75, ((0, 32),))
    w_out = gaussian(streams_of[8], (D, D), (D // 64) ** -0.5, 2.0, ((0, 32),))
    out_bias = gaussian(streams_of[9], (D,), 0.3, 1.75, ((0, 32),))
    ln2_gain = jnp.clip(1.0 + 0.18 * jax.random.normal(streams_of[10], (D,), jnp.float32), 0.099609375, 1.8984375).astype(jnp.bfloat16)
    ln2_bias = gaussian(streams_of[11], (D,), 0.3, 1.75, ((0, 32),))
    w_up = gaussian(streams_of[12], (D, FF), D ** -0.5, 0.25, ((0, 32),))
    up_bias = gaussian(streams_of[13], (FF,), 0.3, 1.75, ((0, 32),))
    w_down = gaussian(streams_of[14], (FF, D), FF ** -0.5, 0.125, ((0, 32),))
    down_bias = gaussian(streams_of[15], (D,), 0.3, 1.75, ((0, 32),))
    cotangent = bell_draw_with(streams_of[16], (ROWS, SLOTS, D), 1.0, 6.0, ((0, 32),), (0, 2, 32, 2.75))
    return dict(inputs=inputs, lengths=lengths, slot_order=slot_order, ln1_gain=ln1_gain, ln1_bias=ln1_bias, w_qkv=w_qkv, q_bias=q_bias, v_bias=v_bias, w_out=w_out, out_bias=out_bias, ln2_gain=ln2_gain, ln2_bias=ln2_bias, w_up=w_up, up_bias=up_bias, w_down=w_down, down_bias=down_bias, cotangent=cotangent)


@jax.custom_vjp
def low(v):
    return lax.optimization_barrier(v.astype(jnp.bfloat16)).astype(jnp.float32)

@jax.custom_vjp
def low_back(v):
    return v

def low_keep(v):
    return (low(v), None)

def low_pass(kept, grad):
    return (grad,)

def back_keep(v):
    return (v, None)

def back_low(kept, grad):
    return (low(grad),)
low.defvjp(low_keep, low_pass)
low_back.defvjp(back_keep, back_low)
epsilon = 1e-05
highest = lax.Precision.HIGHEST

def layer_norm(values, gain, shift):
    centre = lax.optimization_barrier(jnp.mean(values, axis=-1, keepdims=True))
    centred = values - centre
    spread = lax.optimization_barrier(jnp.mean(centred * centred, axis=-1, keepdims=True))
    return centred * lax.rsqrt(spread + epsilon) * gain + shift

def matmul(left, right):
    return jnp.dot(left, right, precision=highest)

def allowed_pairs(lengths, slot_order):
    place = jnp.arange(SLOTS, dtype=jnp.int32)
    valid = place[None, :] < lengths[:, None]
    earlier = slot_order[:, None, :] <= slot_order[:, :, None]
    same = place[:, None] == place[None, :]
    return valid[:, None, :] & earlier | same[None]

def block_forward(params, block_rows, lengths, slot_order):
    ln1_gain, ln1_bias, w_qkv, q_bias, v_bias, w_out, out_bias, ln2_gain, ln2_bias, w_up, up_bias, w_down, down_bias = params
    row_count = block_rows.shape[0]
    flat_rows = block_rows.reshape(row_count * SLOTS, D)
    normed = low(layer_norm(flat_rows, ln1_gain, ln1_bias))
    projected = matmul(normed, w_qkv)
    queries = low(low_back(projected[:, :D] + q_bias))
    keys_proj = low(low_back(projected[:, D:2 * D]))
    values_proj = low(low_back(projected[:, 2 * D:] + v_bias))
    head_shape = (row_count, SLOTS, HEADS, HEAD_DIM)
    queries = queries.reshape(head_shape)
    keys_proj = keys_proj.reshape(head_shape)
    values_proj = values_proj.reshape(head_shape)
    scores = jnp.einsum('rqhd,rkhd->rhqk', queries, keys_proj, precision=highest) * HEAD_DIM ** (-0.5)
    scores = low_back(scores)
    allowed = allowed_pairs(lengths, slot_order)[:, None]
    scores = jnp.where(allowed, scores, -1e+30)
    row_max = lax.optimization_barrier(jnp.max(scores, axis=-1, keepdims=True))
    weights_exp = jnp.exp(scores - row_max)
    probs = weights_exp / lax.optimization_barrier(jnp.sum(weights_exp, axis=-1, keepdims=True))
    mixed = jnp.einsum('rhqk,rkhd->rqhd', low(probs), values_proj, precision=highest)
    mixed = low(low_back(mixed.reshape(row_count * SLOTS, D)))
    attended = low_back(matmul(mixed, w_out) + out_bias)
    middle = flat_rows + attended
    normed_two = low(layer_norm(middle, ln2_gain, ln2_bias))
    up_proj = low_back(matmul(normed_two, w_up) + up_bias)
    activated = low(jax.nn.gelu(up_proj))
    down_proj = low_back(matmul(activated, w_down) + down_bias)
    return (middle + down_proj).reshape(row_count, SLOTS, D)

def reference(inputs, lengths, slot_order, ln1_gain, ln1_bias, w_qkv, q_bias, v_bias, w_out, out_bias, ln2_gain, ln2_bias, w_up, up_bias, w_down, down_bias, cotangent):
    params = tuple((p.astype(jnp.float32) for p in (ln1_gain, ln1_bias, w_qkv, q_bias, v_bias, w_out, out_bias, ln2_gain, ln2_bias, w_up, up_bias, w_down, down_bias)))
    group_rows = 16
    group_count = ROWS // group_rows

    def forward(all_rows, weights):

        def step_fn(member):
            return block_forward(weights, member[0], member[1], member[2])
        shaped = all_rows.reshape(group_count, group_rows, SLOTS, D)
        lens_shaped = lengths.reshape(group_count, group_rows)
        order_shaped = slot_order.reshape(group_count, group_rows, SLOTS)
        result = lax.map(jax.checkpoint(step_fn), (shaped, lens_shaped, order_shaped))
        return result.reshape(ROWS, SLOTS, D)
    result, pullback = jax.vjp(forward, inputs.astype(jnp.float32), params)
    grad_rows, grads = pullback(cotangent.astype(jnp.float32))
    return (result.astype(jnp.bfloat16), grad_rows, grads[0], grads[1], grads[2], grads[3], grads[4], grads[5], grads[6], grads[7], grads[8], grads[9], grads[10], grads[11], grads[12])
```

```python
import functools

import jax
import jax.numpy as jnp
from jax import lax
from jax.experimental import pallas as pl
from jax.experimental.pallas import tpu as pltpu
from jax.sharding import PartitionSpec as P

HEADS = 8
HEAD_DIM = 64
SCALE = HEAD_DIM ** (-0.5)
EPS = 1e-05
MASKED = -1e30
GELU_A = 0.7978845608028654
GELU_B = GELU_A * 0.044715
MESH = pl.DeviceIdType.MESH
BF = jnp.bfloat16
F32 = jnp.float32

D = HEADS * HEAD_DIM
QUADS = 2
QW = D // QUADS
CHUNKS = 4
LN1G, LN1B, QB, VB, OB, LN2G, LN2B, DB, UPB = range(9)


def nn(a, b):
    return lax.dot_general(a, b, (((1,), (0,)), ((), ())), preferred_element_type=F32)


def nt(a, b):
    return lax.dot_general(a, b, (((1,), (1,)), ((), ())), preferred_element_type=F32)


def tn(a, b):
    return lax.dot_general(a, b, (((0,), (0,)), ((), ())), preferred_element_type=F32)


def flip(v):
    return 1 - v


class Gather:
    def __init__(self, buf, send, recv, place):
        self.buf, self.send, self.recv = buf, send, recv
        self.z, self.x, self.y, self.c = place
        self.all = []

    def _go(self, slot, src, dst_dev):
        z, x, y, c = dst_dev
        cp = pltpu.make_async_remote_copy(
            src_ref=src, dst_ref=src, send_sem=self.send.at[slot], recv_sem=self.recv.at[slot],
            device_id=(z * 2 + x, y * 2 + c), device_id_type=MESH)
        cp.start()
        self.all.append(cp)
        return cp

    def along_z(self):
        z, x, y, c = self.z, self.x, self.y, self.c
        own = self.buf.at[z, x * 2 + y, c]
        self.a = [self._go(d - 1, own, (lax.rem(z + d, 4), x, y, c)) for d in (1, 2, 3)]

    def over_xy(self):
        for cp in self.a:
            cp.wait_recv()
        z, x, y, c = self.z, self.x, self.y, self.c
        own = self.buf.at[:, x * 2 + y, c]
        self.b = [
            self._go(3, own, (z, x, flip(y), c)),
            self._go(4, own, (z, flip(x), y, c)),
            self._go(5, own, (z, flip(x), flip(y), c)),
            self._go(6, own, (z, x, y, flip(c))),
        ]

    def to_core(self):
        z, x, y, c = self.z, self.x, self.y, self.c
        self.e = []
        for i, (xx, yy) in enumerate(((x, flip(y)), (flip(x), y), (flip(x), flip(y)))):
            self.b[i].wait_recv()
            self.e.append(self._go(7 + i, self.buf.at[:, xx * 2 + yy, c], (z, x, y, flip(c))))

    def ready(self):
        self.b[3].wait_recv()
        for cp in self.e:
            cp.wait_recv()

    def finish(self):
        for cp in self.all:
            cp.wait_send()


class Scatter:
    def __init__(self, buf, bufs, send, recv, place):
        self.buf = buf
        self.rc, self.rxy, self.s2, self.rz = bufs
        self.send, self.recv = send, recv
        self.z, self.x, self.y, self.c = place
        self.all = []

    def _go(self, slot, src, dst, dst_dev):
        z, x, y, c = dst_dev
        cp = pltpu.make_async_remote_copy(
            src_ref=src, dst_ref=dst, send_sem=self.send.at[slot], recv_sem=self.recv.at[slot],
            device_id=(z * 2 + x, y * 2 + c), device_id_type=MESH)
        cp.start()
        self.all.append(cp)
        return cp

    def to_core(self, zs=None):
        z, x, y, c = self.z, self.x, self.y, self.c
        self.a = self._go(0, self.buf.at[:, :, flip(c)], self.rc, (z, x, y, flip(c)))

    def over_xy(self):
        self.a.wait_recv()
        z, x, y, c = self.z, self.x, self.y, self.c
        n = self.rc.shape[0]

        def add(i, carry):
            self.rc[i] = (self.rc[i].astype(F32) + self.buf[i, :, c].astype(F32)).astype(BF)
            return carry

        lax.fori_loop(0, n, add, 0)
        self.b = [
            self._go(1, self.rc.at[:, x * 2 + flip(y)], self.rxy.at[0], (z, x, flip(y), c)),
            self._go(2, self.rc.at[:, flip(x) * 2 + y], self.rxy.at[1], (z, flip(x), y, c)),
            self._go(3, self.rc.at[:, flip(x) * 2 + flip(y)], self.rxy.at[2], (z, flip(x), flip(y), c)),
        ]

    def along_z(self):
        for cp in self.b:
            cp.wait_recv()
        z, x, y, c = self.z, self.x, self.y, self.c
        self.sum_xy(slice(None))
        self.send_z()

    def sum_xy(self, dst):
        z, x, y, c = self.z, self.x, self.y, self.c
        r = self.rxy
        self.s2[dst] = (
            (self.rc[:, x * 2 + y].astype(F32) + r[0].astype(F32)) + (r[1].astype(F32) + r[2].astype(F32))
        ).astype(BF)

    def send_z(self):
        z, x, y, c = self.z, self.x, self.y, self.c
        self.d = []
        for k in (1, 2, 3):
            to = lax.rem(z + k, 4)
            self.d.append(self._go(3 + k, self.s2.at[to], self.rz.at[k - 1], (to, x, y, c)))

    def result(self):
        for cp in self.d:
            cp.wait_recv()
        r = self.rz
        return (self.s2[self.z].astype(F32) + r[0].astype(F32)) + (r[1].astype(F32) + r[2].astype(F32))

    def finish(self):
        for cp in self.all:
            cp.wait_send()


def layer(comm, rows, slots, ff, *refs):
    tokens = rows * slots
    fc = ff // CHUNKS
    it = iter(refs)
    take = lambda n: [next(it) for _ in range(n)]
    x_hbm, g_hbm, len_ref, ord_ref, vec_in = take(5)
    if comm:
        wqkv_s, wout_s, wup_s, wdn_s = take(4)
    else:
        w_in = take(4 + CHUNKS)
        upb_in, = take(1)
    out_hbm, ig_hbm = take(2)
    if comm:
        gqkv_o, gout_o, gup_o, gdn_o, sg_o = take(5)
    else:
        g_out = take(4 + CHUNKS)
        sg_o, = take(1)
    xv, gv, bias, h1, h1t, pt, mixed, n2, r2, h2, h2t, yacc, dh2, act_s, dpre_s, da, outv, vec, sg = take(19)
    qkv = take(QUADS)
    dproj = take(QUADS)
    w_qkv = take(QUADS)
    w_out, w_dn = take(2)
    w_up = take(CHUNKS)
    g_qkv = take(QUADS)
    g_wout, g_dn = take(2)
    g_up = take(CHUNKS)
    local, = take(1)
    dx1 = yacc

    def tok(r):
        return pl.ds(pl.multiple_of(r * slots, slots), slots)

    def rows_loop(body):
        def step(r, carry):
            body(r)
            return carry

        lax.fori_loop(0, rows, step, 0)

    copies = []

    def start(slot, src, dst):
        cp = pltpu.make_async_copy(src, dst, local.at[slot])
        cp.start()
        return cp

    cx = start(0, x_hbm, xv)
    cg = start(1, g_hbm, gv)
    if comm:
        (small, vplaced, ag_send, ag_recv, rs_send, rs_recv, sm_r, sm_send, sm_recv) = take(9)
        rs_bufs = [take(4) for _ in range(QUADS + 1 + CHUNKS)]
        rs_dn = [take(2) for _ in range(CHUNKS)]
        s2_dn, rz_dn = take(2)
        dp, sh = lax.axis_index("dp"), lax.axis_index("shard")
        z, x, y, c = lax.div(dp, 2), lax.rem(dp, 2), lax.div(sh, 2), lax.rem(sh, 2)
        place = (z, x, y, c)
        xy = x * 2 + y
        lc = []
        k = 2
        for j in range(QUADS):
            for t in range(3):
                lc.append(start(k, wqkv_s.at[:, pl.ds(t * D + j * QW, QW)], w_qkv[j].at[z, xy, c, :, pl.ds(t * QW, QW)]))
                k += 1
        lc.append(start(k, wout_s, w_out.at[z, xy, c])); k += 1
        lc.append(start(k, wdn_s, w_dn.at[z, xy, c])); k += 1
        for j in range(CHUNKS):
            lc.append(start(k, wup_s.at[:, pl.ds(j * fc, fc)], w_up[j].at[z, xy, c])); k += 1
        bar = pltpu.get_barrier_semaphore()
        for zz, xx, yy, cc in [(lax.rem(z + d, 4), x, y, c) for d in (1, 2, 3)] + [
            (z, x, flip(y), c), (z, flip(x), y, c), (z, flip(x), flip(y), c), (z, x, y, flip(c))]:
            pl.semaphore_signal(bar, 1, device_id=(zz * 2 + xx, yy * 2 + cc), device_id_type=MESH)
        row = lax.broadcasted_iota(jnp.int32, (128, 128), 0)
        lane = lax.broadcasted_iota(jnp.int32, (128, 128), 1)
        eye = (lane == row + (xy * 2 + c) * 16).astype(BF)
        eye_up = (lane == row + c * 64).astype(BF)
        v_in = vec_in[...]
        vrow = lax.broadcasted_iota(jnp.int32, (16, 128), 0)
        small[z, xy, c] = jnp.where(vrow == UPB, nn(v_in, eye_up), nn(v_in, eye)).astype(BF)
        gathers = [
            Gather(b, ag_send.at[i], ag_recv.at[i], place)
            for i, b in enumerate([small] + w_qkv + [w_out, w_dn] + w_up)
        ]
        pl.semaphore_wait(bar, 7)
        gathers[0].along_z()
        for cp in lc:
            cp.wait()
        for gth in gathers[1:]:
            gth.along_z()
        gathers[0].over_xy()
        gathers[1].over_xy()
    else:
        lc = [start(2 + i, w_in[i], b) for i, b in enumerate(w_qkv + [w_out, w_dn] + w_up)]

    kk = lax.broadcasted_iota(jnp.int32, (slots, slots), 0)
    qq = lax.broadcasted_iota(jnp.int32, (slots, slots), 1)
    for r in range(rows):
        across = jnp.broadcast_to(ord_ref[r : r + 1, :].astype(F32), (slots, slots))
        down = across.T
        ok = jnp.logical_or(jnp.logical_and(kk < len_ref[r], down <= across), kk == qq)
        bias[r] = jnp.where(ok, 0.0, MASKED)
    sg[...] = jnp.zeros_like(sg)
    cx.wait()
    if comm:
        gathers[0].to_core()
        gathers[1].to_core()
        gathers[2].over_xy()
        gathers[0].ready()
        acc = None
        for zz in range(4):
            tot = None
            for w in range(4):
                for q in range(2):
                    b = small[zz, w, q].astype(F32)
                    tot = b if tot is None else tot + b
            vec[0:16, zz * 128 : (zz + 1) * 128] = tot
            for w in range(4):
                two = (small[zz, w, 0].astype(F32) + small[zz, w, 1].astype(F32))[UPB : UPB + 1]
                vec[16 + zz : 17 + zz, w * 128 : (w + 1) * 128] = two
    else:
        vec[0:16] = vec_in[...]
        vec[16:20] = upb_in[...]

    def v(i):
        return vec[i : i + 1, :]

    def add(i, val):
        sg[i : i + 1, :] += val

    def col(val):
        return jnp.sum(val, axis=0, keepdims=True)

    def norm(val):
        centred = val - jnp.mean(val, axis=-1, keepdims=True)
        spread = jnp.mean(centred * centred, axis=-1, keepdims=True)
        r = lax.rsqrt(spread + EPS)
        return centred * r, r

    def first_norm(r):
        t = tok(r)
        n, _ = norm(xv[t].astype(F32))
        h = (n * v(LN1G) + v(LN1B)).astype(BF)
        h1[t] = h
        h1t[:, t] = h.T

    rows_loop(first_norm)
    lane = lax.broadcasted_iota(jnp.int32, (slots, 128), 1)
    first = lane < HEAD_DIM

    def heads_apart(pair):
        nil = jnp.zeros_like(pair)
        return jnp.where(first, pair, nil), jnp.where(first, nil, pair)

    for j in range(QUADS):
        if comm:
            if j + 1 < QUADS:
                gathers[1 + j + 1].to_core()
            if j == 0:
                gathers[3].over_xy()
                gathers[4].over_xy()
            else:
                gathers[5].over_xy()
            gathers[1 + j].ready()
        else:
            lc[j].wait()
        shift = jnp.concatenate(
            [v(QB)[:, j * QW : (j + 1) * QW], jnp.zeros((1, QW), F32), v(VB)[:, j * QW : (j + 1) * QW]], axis=1)
        mult = jnp.where(lax.broadcasted_iota(jnp.int32, (1, 3 * QW), 1) < QW, SCALE, 1.0)

        def attend(r, j=j, shift=shift, mult=mult):
            t = tok(r)
            w = w_qkv[j][...].reshape(D, 3 * QW)
            proj = ((nn(h1[t], w) + shift) * mult).astype(BF)
            qkv[j][t] = proj
            for p in range(QW // 128):
                s = slice(p * 128, (p + 1) * 128)
                q = proj[:, p * 128 : (p + 1) * 128]
                k = proj[:, QW + p * 128 : QW + (p + 1) * 128]
                u = proj[:, 2 * QW + p * 128 : 2 * QW + (p + 1) * 128]
                sc = nt(jnp.concatenate(heads_apart(k), axis=0), q)
                ps = []
                for h in range(2):
                    sh_ = sc[h * slots : (h + 1) * slots] + bias[r]
                    e = jnp.exp(sh_ - jnp.max(sh_, axis=0, keepdims=True))
                    ps.append((e * (1.0 / jnp.sum(e, axis=0, keepdims=True))).astype(BF))
                probs = jnp.concatenate(ps, axis=0)
                pt[j, r, p] = probs
                m = tn(probs, jnp.concatenate(heads_apart(u), axis=0))
                mixed[t, pl.ds(j * QW + p * 128, 128)] = m.astype(BF)

        rows_loop(attend)

    cg.wait()
    if comm:
        gathers[3].to_core()
        gathers[4].to_core()
        gathers[6].over_xy()
        gathers[3].ready()
    else:
        lc[QUADS].wait()

    def second_norm(r):
        t = tok(r)
        x1 = xv[t].astype(F32) + (nn(mixed[t], w_out[...].reshape(D, D)) + v(OB))
        n, rr = norm(x1)
        h = (n * v(LN2G) + v(LN2B)).astype(BF)
        h2[t] = h
        h2t[:, t] = h.T
        n2[t] = n
        r2[t] = jnp.broadcast_to(rr, (slots, 128))
        yacc[t] = x1 + v(DB)
        dh2[t] = jnp.zeros((slots, D), F32)
        add(DB, col(gv[t].astype(F32)))

    rows_loop(second_norm)
    if comm:
        gathers[4].ready()
        gathers[5].to_core()
        gathers[6].to_core()
        gathers[7].over_xy()
        gathers[8].over_xy()
        sc = []
    else:
        lc[QUADS + 1].wait()

    for j in range(CHUNKS):
        if comm:
            gathers[5 + j].ready()
            if j == 1:
                gathers[7].to_core()
                gathers[8].to_core()
        else:
            lc[QUADS + 2 + j].wait()
        ub = vec[16 + j : 17 + j, :]

        def feed(r, j=j, ub=ub):
            t = tok(r)
            wu = w_up[j][...].reshape(D, fc)
            wd = w_dn[j].reshape(fc, D)
            pre = nn(h2[t], wu) + ub
            sq = pre * pre
            th = jnp.tanh(pre * (GELU_A + GELU_B * sq))
            half = 0.5 * pre
            a = (half + half * th).astype(BF)
            slope = (0.5 + 0.5 * th) + half * (1.0 - th * th) * (GELU_A + 3.0 * GELU_B * sq)
            dpre = nt(gv[t], wd) * slope
            dl = dpre.astype(BF)
            act_s[t] = a
            dpre_s[t] = dl
            add(12 + j, col(dpre))
            yacc[t] += nn(a, wd)
            dh2[t] += nt(dl, wu)

        rows_loop(feed)
        g_dn[j] = tn(act_s[...], gv[...]).astype(BF).reshape(g_dn.shape[1:])
        g_up[j][...] = nn(h2t[...], dpre_s[...]).astype(BF).reshape(g_up[j].shape)
        if comm:
            up = Scatter(g_up[j], rs_bufs[QUADS + 1 + j], rs_send.at[j], rs_recv.at[j], place)
            dn = Scatter(g_dn.at[pl.ds(j, 1)], (rs_dn[j][0], rs_dn[j][1], s2_dn, rz_dn),
                         rs_send.at[CHUNKS + j], rs_recv.at[CHUNKS + j], place)
            up.to_core()
            dn.to_core()
            sc.append((up, dn))
            if j >= 1:
                sc[j - 1][0].over_xy()
                sc[j - 1][1].over_xy()
            if j >= 2:
                sc[j - 2][0].along_z()

    def second_back(r):
        t = tok(r)
        outv[t] = yacc[t].astype(BF)
        g2 = dh2[t]
        n = n2[t]
        add(LN2G, col(g2 * n))
        add(LN2B, col(g2))
        e = g2 * v(LN2G)
        dx = gv[t].astype(F32) + r2[t, pl.ds(0, 1)] * (
            e - jnp.mean(e, axis=-1, keepdims=True) - n * jnp.mean(e * n, axis=-1, keepdims=True))
        dx1[t] = dx
        add(OB, col(dx))
        da[t] = dx.astype(BF)

    rows_loop(second_back)
    co = start(0, outv, out_hbm)
    g_wout[...] = tn(mixed[...], da[...]).astype(BF).reshape(g_wout.shape)
    if comm:
        last = len(sc) - 1
        sc[last][0].over_xy()
        sc[last][1].over_xy()
        sc[last - 1][0].along_z()
        wo = Scatter(g_wout, rs_bufs[QUADS], rs_send.at[2 * CHUNKS], rs_recv.at[2 * CHUNKS], place)
        wo.to_core()
        sq_ = []

    for j in range(QUADS):
        def back(r, j=j):
            t = tok(r)
            wo_ = w_out[2 * j : 2 * j + 2].reshape(QW, D)
            dmix = nt(da[t], wo_).astype(BF)
            for p in range(QW // 128):
                q = qkv[j][t, pl.ds(p * 128, 128)]
                k = qkv[j][t, pl.ds(QW + p * 128, 128)]
                u = qkv[j][t, pl.ds(2 * QW + p * 128, 128)]
                dm = dmix[:, p * 128 : (p + 1) * 128]
                probs = pt[j, r, p]
                dm0, dm1 = heads_apart(dm)
                q0, q1 = heads_apart(q)
                dv = nn(probs[:slots], dm0) + nn(probs[slots:], dm1)
                dpt = nt(jnp.concatenate(heads_apart(u), axis=0), dm)
                ds = []
                for h in range(2):
                    pf = probs[h * slots : (h + 1) * slots].astype(F32)
                    d = dpt[h * slots : (h + 1) * slots]
                    ds.append((pf * (d - jnp.sum(pf * d, axis=0, keepdims=True))).astype(BF))
                dk = nn(ds[0], q0) + nn(ds[1], q1)
                dq = tn(jnp.concatenate(ds, axis=0), jnp.concatenate(heads_apart(k), axis=0)) * SCALE
                s0 = j * QW + p * 128
                sg[QB : QB + 1, s0 : s0 + 128] += col(dq)
                sg[VB : VB + 1, s0 : s0 + 128] += col(dv)
                dproj[j][t, pl.ds(p * 128, 128)] = dq.astype(BF)
                dproj[j][t, pl.ds(QW + p * 128, 128)] = dk.astype(BF)
                dproj[j][t, pl.ds(2 * QW + p * 128, 128)] = dv.astype(BF)

        rows_loop(back)
        g_qkv[j][...] = nn(h1t[...], dproj[j][...]).astype(BF).reshape(g_qkv[j].shape)
        if comm:
            one = Scatter(g_qkv[j], rs_bufs[j], rs_send.at[2 * CHUNKS + 1 + j], rs_recv.at[2 * CHUNKS + 1 + j], place)
            one.to_core()
            sq_.append(one)
            if j == 0:
                sc[last][0].along_z()
                for i, (_, dn) in enumerate(sc):
                    for cp in dn.b:
                        cp.wait_recv()
                    dn.sum_xy(pl.ds(i, 1))
                sc[last][1].send_z()
                wo.over_xy()
            else:
                sq_[0].over_xy()
                wo.along_z()
                sq_[1].over_xy()
                sq_[0].along_z()

    def first_back(r):
        t = tok(r)
        g1 = nt(dproj[0][t], w_qkv[0][...].reshape(D, 3 * QW)) + nt(dproj[1][t], w_qkv[1][...].reshape(D, 3 * QW))
        n, rr = norm(xv[t].astype(F32))
        add(LN1G, col(g1 * n))
        add(LN1B, col(g1))
        e = g1 * v(LN1G)
        dx1[t] = dx1[t] + rr * (e - jnp.mean(e, axis=-1, keepdims=True) - n * jnp.mean(e * n, axis=-1, keepdims=True))

    rows_loop(first_back)
    ci = start(1, dx1, ig_hbm)
    if comm:
        sends = []

        def swap(slot, dev):
            zz, xx, yy, cc = dev
            cp = pltpu.make_async_remote_copy(
                src_ref=sg_src.at[slot_src], dst_ref=sm_r.at[slot], send_sem=sm_send.at[slot], recv_sem=sm_recv.at[slot],
                device_id=(zz * 2 + xx, yy * 2 + cc), device_id_type=MESH)
            cp.start()
            sends.append(cp)
            return cp

        sg_src = sm_r
        slot_src = 7
        sm_r[7] = sg[...]
        one_ = swap(0, (z, x, y, flip(c)))
        one_.wait_recv()
        slot_src = 8
        sm_r[8] = sm_r[7] + sm_r[0]
        three = [swap(1, (z, x, flip(y), c)), swap(2, (z, flip(x), y, c)), swap(3, (z, flip(x), flip(y), c))]
        sq_[1].along_z()
        for cp in three:
            cp.wait_recv()
        slot_src = 9
        sm_r[9] = (sm_r[8] + sm_r[1]) + (sm_r[2] + sm_r[3])
        three = [swap(3 + k, (lax.rem(z + k, 4), x, y, c)) for k in (1, 2, 3)]
        for j in range(CHUNKS):
            gup_o[:, j * fc : (j + 1) * fc] = sc[j][0].result()
        gdn_o[...] = sc[last][1].result()
        gout_o[...] = wo.result()
        for j in range(QUADS):
            res = sq_[j].result()
            for t in range(3):
                gqkv_o[:, t * D + j * QW : t * D + (j + 1) * QW] = res[:, t * QW : (t + 1) * QW]
        for cp in three:
            cp.wait_recv()
        sg_o[...] = (sm_r[9] + sm_r[4]) + (sm_r[5] + sm_r[6])
        for gth in gathers:
            gth.finish()
        for up, dn in sc:
            up.finish()
            dn.finish()
        wo.finish()
        for one in sq_:
            one.finish()
        for cp in sends:
            cp.wait_send()
    else:
        sg_o[...] = sg[...]
        out_c = [start(2 + i, b, o) for i, (b, o) in enumerate(zip(g_qkv + [g_wout, g_dn] + g_up, g_out))]
        for cp in out_c:
            cp.wait()
    co.wait()
    ci.wait()


def run_layer(comm, rows, slots, ff, operands):
    tokens = rows * slots
    fc = ff // CHUNKS
    blk = lambda r, c: (4, 4, 2, r, c)
    pieces = [blk(D // 32, 3 * QW)] * QUADS + [blk(D // 32, D), blk(ff // 32, D)] + [blk(D // 32, fc)] * CHUNKS
    any_ = pl.BlockSpec(memory_space=pl.ANY)
    vm = pl.BlockSpec(memory_space=pltpu.VMEM)
    smem = pl.BlockSpec(memory_space=pltpu.SMEM)
    in_specs = [any_, any_, smem, vm, vm]
    out_shape = [jax.ShapeDtypeStruct((tokens, D), BF), jax.ShapeDtypeStruct((tokens, D), F32)]
    out_specs = [any_, any_]
    if comm:
        in_specs += [any_] * 4
        out_shape += [jax.ShapeDtypeStruct(s, F32) for s in ((D // 32, 3 * D), (D // 32, D), (D // 32, ff), (ff // 32, D))]
        out_specs += [vm] * 4
    else:
        in_specs += [any_] * len(pieces) + [vm]
        out_shape += [jax.ShapeDtypeStruct(s, BF) for s in pieces]
        out_specs += [any_] * len(pieces)
    out_shape.append(jax.ShapeDtypeStruct((16, D), F32))
    out_specs.append(vm)
    V = pltpu.VMEM
    scratch = [
        V((tokens, D), BF), V((tokens, D), BF), V((rows, slots, slots), F32), V((tokens, D), BF), V((D, tokens), BF),
        V((QUADS, rows, QW // 128, 2 * slots, slots), BF), V((tokens, D), BF), V((tokens, D), F32), V((tokens, 128), F32),
        V((tokens, D), BF), V((D, tokens), BF), V((tokens, D), F32), V((tokens, D), F32), V((tokens, fc), BF),
        V((tokens, fc), BF), V((tokens, D), BF), V((tokens, D), BF), V((24, D), F32), V((16, D), F32),
    ]
    scratch += [V((tokens, 3 * QW), BF)] * (2 * QUADS)
    scratch += [V(s, BF) for s in pieces] * 2
    scratch += [pltpu.SemaphoreType.DMA((24,))]
    if comm:
        n_ag, n_rs = len(pieces) + 1, 2 * CHUNKS + 1 + QUADS
        dma = pltpu.SemaphoreType.DMA
        scratch += [V(blk(16, 128), BF), V((16, 128), BF), dma((n_ag, 10)), dma((n_ag, 10)), dma((n_rs, 7)), dma((n_rs, 7)),
                    V((10, 16, D), F32), dma((7,)), dma((7,))]
        for s in pieces[:QUADS] + [pieces[QUADS]] + pieces[QUADS + 2 :]:
            r, c = s[3:]
            scratch += [V((4, 4, r, c), BF), V((3, 4, r, c), BF), V((4, r, c), BF), V((3, r, c), BF)]
        r, c = pieces[QUADS + 1][3:]
        for _ in range(CHUNKS):
            scratch += [V((1, 4, r, c), BF), V((3, 1, r, c), BF)]
        scratch += [V((4, r, c), BF), V((3, r, c), BF)]
    return pl.pallas_call(
        functools.partial(layer, comm, rows, slots, ff),
        out_shape=out_shape, in_specs=in_specs, out_specs=out_specs, scratch_shapes=scratch,
        compiler_params=pltpu.CompilerParams(
            vmem_limit_bytes=63 << 20, **(dict(collective_id=0, has_side_effects=True) if comm else {})),
        cost_estimate=pl.CostEstimate(flops=22_000_000_000, bytes_accessed=6 << 20, transcendentals=4 << 20),
    )(*operands)


def shards(
    inputs, lengths, slot_order, ln1_gain, ln1_bias, w_qkv, q_bias, v_bias, w_out, out_bias, ln2_gain, ln2_bias, w_up, up_bias,
    w_down, down_bias, cotangent, fast=True,
):
    rows, slots, width = inputs.shape
    tokens = rows * slots
    flat = (inputs.reshape(tokens, width), cotangent.reshape(tokens, width), lengths, slot_order)
    vectors = [ln1_gain, ln1_bias, q_bias, v_bias, out_bias, ln2_gain, ln2_bias, down_bias, up_bias]
    axes = ("dp", "shard")
    me = lax.axis_index(axes)
    n = lax.axis_size(axes)
    if fast:
        ff = w_up.shape[1]
        packed = jnp.stack([jnp.pad(a, (0, 128 - a.shape[0])) for a in vectors] + [jnp.zeros((128,), BF)] * 7)
        out, ig, gqkv, gout, gup, gdn, sg = run_layer(
            True, rows, slots, ff, flat + (packed, w_qkv, w_out, w_up, w_down))
        mine = lax.dynamic_slice(sg, (0, me * (width // n)), (8, width // n))
        upb = lax.dynamic_slice(sg[12:16].reshape(-1), (me * (ff // n),), (ff // n,))
    else:
        ff = w_up.shape[1]
        full = lambda a: lax.all_gather(a, axes, axis=0, tiled=True)
        whole = [full(a).astype(F32) for a in vectors]
        packed = jnp.stack(whole[:8] + [jnp.zeros((width,), F32)] * 8)
        wq, wo, wu, wd = full(w_qkv), full(w_out), full(w_up), full(w_down)
        fc = ff // CHUNKS
        cut = lambda a: a.reshape(4, 4, 2, a.shape[0] // 32, a.shape[1])
        pieces = [cut(jnp.concatenate([wq[:, t * D + j * QW : t * D + (j + 1) * QW] for t in range(3)], axis=1)) for j in range(QUADS)]
        pieces += [cut(wo), cut(wd)] + [cut(wu[:, j * fc : (j + 1) * fc]) for j in range(CHUNKS)]
        res = run_layer(False, rows, slots, ff, flat + (packed, *pieces, whole[8].reshape(CHUNKS, fc)))
        out, ig, sg = res[0], res[1], res[-1]
        back = [r.astype(F32).reshape(-1, r.shape[-1]) for r in res[2:-1]]
        own = lambda a: lax.psum_scatter(a, axes, scatter_dimension=0, tiled=True)
        gq = jnp.stack(back[:QUADS]).reshape(QUADS, D, 3, QW).transpose(1, 2, 0, 3).reshape(D, 3 * D)
        gqkv, gout, gdn, gup = own(gq), own(back[QUADS]), own(back[QUADS + 1]), own(jnp.concatenate(back[QUADS + 2 :], axis=1))
        mine = own(sg[0:8].T).T
        upb = own(sg[12:16].reshape(-1))
    shape = (rows, slots, width)
    return (
        out.reshape(shape), ig.reshape(shape), mine[LN1G], mine[LN1B], gqkv, mine[QB], mine[VB], gout, mine[OB], mine[LN2G],
        mine[LN2B], gup, upb, gdn, mine[DB],
    )


def solution(mesh):
    whole = P(("dp", "shard"))
    fast = mesh.shape["dp"] == 8 and mesh.shape["shard"] == 4
    return jax.shard_map(
        functools.partial(shards, fast=fast), mesh=mesh, in_specs=(whole,) * 17, out_specs=(whole,) * 15, check_vma=False)
```

```python
import functools
import types

import jax
import jax.numpy as jnp
from jax import lax
from jax.experimental import pallas as pl
from jax.experimental.pallas import tpu as pltpu
from jax.sharding import PartitionSpec as P

HEADS = 8
HEAD_DIM = 64
SCALE = HEAD_DIM ** (-0.5)
EPS = 1e-05
MASKED = -1e30
GELU_A = 0.7978845608028654
GELU_B = GELU_A * 0.044715
MESH = pl.DeviceIdType.MESH
BF = jnp.bfloat16
F32 = jnp.float32

D = HEADS * HEAD_DIM
GROUPS = ((0, 256), (256, 256))
CHUNKS = 4
LN1G, LN1B, QB, VB, OB, LN2G, LN2B, DB, UPB = range(9)
LATE = (LN1G, LN1B, QB, VB)
EARLY = (OB, LN2G, LN2B, DB)


def nn(a, b):
    return lax.dot_general(a, b, (((1,), (0,)), ((), ())), preferred_element_type=F32)


def nt(a, b):
    return lax.dot_general(a, b, (((1,), (1,)), ((), ())), preferred_element_type=F32)


def tn(a, b):
    return lax.dot_general(a, b, (((0,), (0,)), ((), ())), preferred_element_type=F32)


def nothing():
    pass


class Node:
    def __getattr__(self, name):
        return nothing


def plan(x):
    return types.SimpleNamespace(
        start=(x.sm.zgo, x.g[0].zgo, x.g[1].zgo, x.out.zgo, x.u[0].zgo, x.dn.zgo, x.u[1].zgo, x.u[2].zgo, x.u[3].zgo,),
        pre=(x.sm.xy, x.g[0].xy, x.sm.turn, x.sm.core, x.sm.ready,),
        proj=(x.g[1].xy, x.out.xy, x.g[0].turn, x.u[0].xy, x.g[0].core, x.g[0].ready, x.g[1].turn, x.d[0].xy, x.out.turn, x.u[1].xy, x.d[1].xy, x.g[1].core, x.g[1].ready,),
        attend={0: (x.u[0].turn, x.u[2].xy,), 1: (x.out.core, x.d[0].turn, x.u[1].turn, x.d[2].xy, x.u[3].xy,)},
        second_norm={0: (x.out.ready, x.u[0].core, x.d[1].turn, x.u[2].turn, x.d[3].xy, x.d[0].core,), 1: (x.u[1].core,)},
        feed=(
            {0: (x.u[0].ready, x.d[0].ready,), 1: (x.d[2].turn,)},
            {0: (x.u[1].ready, x.d[1].ready,), 1: (x.d[2].core, x.d[3].turn,)},
            {0: (x.u[2].ready, x.d[2].ready,), 1: (x.d[3].core, x.sd[0].xy,)},
            {0: (x.u[3].ready, x.d[3].ready,), 1: (x.sd[0].turn, x.sd[1].xy,)},
        ),
        fed=((x.d[1].core, x.u[3].turn, x.u[2].core,), (x.u[3].core, x.sd[0].core, x.su[0].core,), (x.su[0].xy, x.sd[1].core, x.su[1].core,), (x.su[0].turn, x.su[1].xy, x.sd[2].core, x.su[2].core,)),
        gdn=(),
        gup=(x.sd[0].sum, x.sd[3].core,),
        second_back={0: (x.sd[1].turn, x.sd[2].xy, x.su[3].core,), 1: (x.su[2].xy,)},
        gwout=(x.te.go, x.su[0].sum, x.su[1].turn, x.sd[3].xy, x.su[3].xy,),
        back=({0: (x.su[3].turn, x.sq[1].core, x.te.end,), 1: (x.sd[2].sum, x.su[2].sum, x.so.turn, x.sq[1].xy,)}, {0: (x.so.core,), 1: (x.sd[1].sum, x.sd[2].turn, x.su[2].turn, x.so.xy, x.te.turn,)}),
        gqkv=((x.sd[3].sum, x.su[3].sum, x.su[1].end,), (x.su[1].sum, x.sd[3].turn, x.su[0].end,)),
        first_back={0: (x.so.sum, x.sq[0].core,), 1: (x.sq[0].xy, x.su[2].end,)},
        tail=(x.tl.go, x.sq[1].sum, x.tl.turn, x.sq[0].sum, x.su[3].end, x.dw.end, x.so.end, x.sq[1].end, x.tl.end, x.sq[0].end,),
    )


def direct_of(x):
    return (x.sm, x.g[0], x.sq[0], x.sq[1],)


def scatter_direct(n_groups):
    return (0, 1,)


class Place:
    def __init__(self):
        dp, sh = lax.axis_index("dp"), lax.axis_index("shard")
        self.z, x, y, self.c = lax.div(dp, 2), lax.rem(dp, 2), lax.div(sh, 2), lax.rem(sh, 2)
        nx, ny, self.nc = 1 - x, 1 - y, 1 - self.c
        self.own, self.ix, self.iy, self.id = x * 2 + y, nx * 2 + y, x * 2 + ny, nx * 2 + ny
        self.zs = [lax.rem(self.z + k, 4) for k in (1, 2, 3)]
        at = lambda z, x, y, c: (z * 2 + x, y * 2 + c)
        self.dev_z = [at(k, x, y, self.c) for k in self.zs]
        self.dev_x, self.dev_y = at(self.z, nx, y, self.c), at(self.z, x, ny, self.c)
        self.dev_d, self.dev_c = at(self.z, nx, ny, self.c), at(self.z, x, y, self.nc)
        self.others = [self.dev_x, self.dev_y, self.dev_d, self.dev_c, at(self.z, nx, y, self.nc), at(self.z, x, ny, self.nc),
                       at(self.z, nx, ny, self.nc)]
        self.bytes = {}

    def send(self, src, dst, out, land, device):
        at = lambda pair: pair[0].at[pair[1]]
        cp = pltpu.make_async_remote_copy(
            src_ref=at(src), dst_ref=at(dst), send_sem=at(out), recv_sem=at(land), device_id=device, device_id_type=MESH)
        cp.start()
        n = 1
        for k in cp.src_ref.shape:
            n *= k
        key = (id(out[0]), *out[1])
        self.bytes[key] = self.bytes.get(key, 0) + n * jnp.dtype(cp.src_ref.dtype).itemsize


ALL = slice(None)
TWO, THREE, FOUR = pl.ds(0, 2), pl.ds(0, 3), pl.ds(0, 4)


def wait_for(like, sem):
    ref = like[0].at[like[1]]
    pltpu.make_async_copy(ref, ref, sem[0].at[sem[1]]).wait()


class GatherZ:
    def __init__(self, me, buf, out, land):
        self.me, self.buf, self.out, self.land = me, buf, out, land

    def go(self):
        me = self.me
        own = (self.buf, (me.z, me.own, me.c))
        for k in range(3):
            me.send(own, own, self.out, self.land, me.dev_z[k])

    def wait(self):
        wait_for((self.buf, (THREE, 0, 0)), self.land)


class Gather:
    def __init__(self, me, buf, outs, land, direct=False, zs=ALL):
        self.me, self.buf, self.direct, self.zs = me, buf, direct, zs
        self.out, self.out_core = outs
        self.land = [(land[0], (*land[1], k)) for k in range(3)]

    def line(self, i, cols=None):
        return self.buf, (self.zs, i, self.me.c) + (() if cols is None else (ALL, cols))

    def to(self, line, k, device):
        self.me.send(line, line, self.out_core if k == 2 else self.out, self.land[k], device)

    def xy(self):
        me, own = self.me, self.line(self.me.own)
        self.to(own, 0, me.dev_x)
        self.to(own, 0, me.dev_y)
        if self.direct:
            self.to(own, 1, me.dev_d)
        self.to(own, 2, me.dev_c)

    def turn(self):
        me = self.me
        wait_for((self.buf, (self.zs, TWO, 0)), self.land[0])
        if not self.direct:
            h = self.buf.shape[-1] // 2
            self.to(self.line(me.ix, pl.ds(0, h)), 1, me.dev_y)
            self.to(self.line(me.iy, pl.ds(h, h)), 1, me.dev_x)
        self.to(self.line(me.ix), 2, me.dev_c)
        self.to(self.line(me.iy), 2, me.dev_c)

    def core(self):
        wait_for((self.buf, (self.zs, 0, 0)), self.land[1])
        self.to(self.line(self.me.id), 2, self.me.dev_c)

    def ready(self):
        wait_for((self.buf, (self.zs, FOUR, 0)), self.land[2])


class Scatter:
    def __init__(self, me, buf, bufs, outs, land, direct=False, zs=ALL):
        self.me, self.buf, self.direct, self.zs = me, buf, direct, zs
        self.out_core, self.out = outs
        self.rc, self.r1, self.r2, self.s2 = bufs
        self.land = [(land[0], (*land[1], k)) for k in range(3)]
        self.h = buf.shape[-1] // 2

    def core(self):
        me = self.me
        me.send((self.buf, (self.zs, ALL, me.nc)), (self.rc, (ALL,)), self.out_core, self.land[0], me.dev_c)

    def to(self, where, cols, dst, k, device):
        me = self.me
        me.send((self.rc, (ALL, where) + (() if cols is None else (ALL, cols))), dst, self.out, self.land[k], device)

    def xy(self):
        me, h, rc, r1, r2 = self.me, self.h, self.rc, self.r1, self.r2
        wait_for((rc, (ALL,)), self.land[0])
        first = 0 if self.zs == ALL else self.zs.start
        for i in range(rc.shape[0]):
            rc[i] = rc[i] + self.buf[first + i, :, me.c]
        if self.direct:
            self.to(me.ix, None, (r2, (0,)), 2, me.dev_x)
            self.to(me.iy, None, (r2, (1,)), 2, me.dev_y)
            self.to(me.id, None, (r1, (ALL,)), 2, me.dev_d)
        else:
            lo, hi = pl.ds(0, h), pl.ds(h, h)
            self.to(me.id, lo, (r1, (0,)), 1, me.dev_x)
            self.to(me.id, hi, (r1, (1,)), 1, me.dev_y)
            self.to(me.ix, lo, (r2, (0, ALL, ALL, lo)), 2, me.dev_x)
            self.to(me.iy, hi, (r2, (1, ALL, ALL, hi)), 2, me.dev_y)

    def turn(self):
        me, h, rc, r1, r2 = self.me, self.h, self.rc, self.r1, self.r2
        wait_for((r1, (ALL,)), self.land[1])
        rc[:, me.iy, :, :h] = rc[:, me.iy, :, :h] + r1[0]
        rc[:, me.ix, :, h:] = rc[:, me.ix, :, h:] + r1[1]
        lo, hi = pl.ds(0, h), pl.ds(h, h)
        self.to(me.iy, lo, (r2, (1, ALL, ALL, lo)), 2, me.dev_y)
        self.to(me.ix, hi, (r2, (0, ALL, ALL, hi)), 2, me.dev_x)

    def sum(self):
        f = lambda v: v.astype(F32)
        if self.direct:
            wait_for((self.rc, (ALL, THREE)), self.land[2])
        else:
            wait_for((self.r2, (ALL,)), self.land[2])
        tot = f(self.rc[:, self.me.own]) + (f(self.r2[0]) + f(self.r2[1]))
        if self.direct:
            tot = tot + f(self.r1[...])
        self.s2[self.zs] = tot.astype(BF)


class ScatterZ:
    def __init__(self, me, s2, rz, out, land):
        self.me, self.s2, self.rz, self.out, self.land = me, s2, rz, out, land

    def go(self):
        me = self.me
        for k in range(3):
            me.send((self.s2, (me.zs[k],)), (self.rz, (k,)), self.out, self.land, me.dev_z[k])

    def result(self):
        wait_for((self.rz, (ALL,)), self.land)
        f = lambda v: v.astype(F32)
        return (f(self.s2[self.me.z]) + f(self.rz[0])) + (f(self.rz[1]) + f(self.rz[2]))


class Total:
    def __init__(self, me, buf, sems):
        self.me, self.buf = me, buf
        self.sem = [(sems, (k,)) for k in range(4)]

    def go(self):
        for i, d in enumerate(self.me.others):
            self.me.send((self.buf, (0,)), (self.buf, (2 + i,)), self.sem[0], self.sem[1], d)

    def turn(self):
        me, b = self.me, self.buf
        wait_for((b, (pl.ds(2, 7),)), self.sem[1])
        b[1] = ((b[0] + b[2]) + (b[3] + b[4])) + ((b[5] + b[6]) + (b[7] + b[8]))
        for k in range(3):
            me.send((b, (1,)), (b, (9 + k,)), self.sem[2], self.sem[3], me.dev_z[k])

    def result(self):
        b = self.buf
        wait_for((b, (pl.ds(9, 3),)), self.sem[3])
        return (b[1] + b[9]) + (b[10] + b[11])

    def finish(self):
        wait_for((self.buf, (pl.ds(2, 7),)), self.sem[0])
        wait_for((self.buf, (pl.ds(9, 3),)), self.sem[2])


def layer(comm, rows, slots, ff, *refs):
    tokens = rows * slots
    fc = ff // CHUNKS
    it = iter(refs)
    take = lambda n: [next(it) for _ in range(n)]
    n_groups = len(GROUPS)
    n_pieces = n_groups + 2 + CHUNKS
    x_hbm, g_hbm, len_ref, ord_ref = take(4)
    if comm:
        vec_in = take(9)
        wqkv_s, wout_s, wup_s, wdn_s = take(4)
    else:
        vec_in, = take(1)
        w_in = take(n_pieces)
        upb_in, = take(1)
    out_hbm, ig_hbm = take(2)
    if comm:
        gqkv_o, gout_o, gup_o, gdn_o, sg_o, upb_o = take(6)
    else:
        g_out = take(n_pieces)
        sg_o, = take(1)
    xv, gv, bias, h1, h1t, pt, mixed, n2, r2, h2, h2t, x1v, dx1, dh2, act, dpre_s, da, outv, vec, sg = take(20)
    qkv = take(n_groups)
    dproj = take(n_groups)
    w_qkv = take(n_groups)
    w_out, w_dn = take(2)
    w_up = take(CHUNKS)
    g_qkv = take(n_groups)
    g_wout, g_dn = take(2)
    g_up = take(CHUNKS)
    local, = take(1)
    x = types.SimpleNamespace(
        sm=Node(), g=[Node() for _ in GROUPS], out=Node(), dn=Node(), u=[Node() for _ in range(CHUNKS)], d=[Node() for _ in range(CHUNKS)],
        sq=[Node() for _ in GROUPS], so=Node(), su=[Node() for _ in range(CHUNKS)], sd=[Node() for _ in range(CHUNKS)], dw=Node(),
        te=Node(), tl=Node())

    def tok(r):
        return pl.ds(pl.multiple_of(r * slots, slots), slots)

    def now(todo):
        for f in todo:
            f()

    def rows_loop(body, ticks={}, unroll=1, also=None):
        def step(i, carry):
            if comm:
                for k in ticks:

                    @pl.when(i == k)
                    def _(k=k):
                        now(ticks[k])

            for u in range(unroll):
                body(i * unroll + u)
            if also is not None:
                also(i)
            return carry

        lax.fori_loop(0, rows // unroll, step, 0)

    def start(slot, src, dst):
        cp = pltpu.make_async_copy(src, dst, local.at[slot])
        cp.start()
        return cp

    cx = start(0, x_hbm, xv)
    cg = start(1, g_hbm, gv)
    if comm:
        small, early, late, sem_out, sem_z, sem_x, sem_s, sem_sz, sem_e, sem_l = take(10)
        rs_bufs = [take(4) for _ in range(n_groups + 1 + CHUNKS)]
        dn_bufs = [take(3) for _ in range(CHUNKS)]
        s2_dn, = take(1)
        rzs = take(n_groups + 2 + CHUNKS)
        me = Place()
        mine = (me.z, me.own, me.c)
        bar = pltpu.get_barrier_semaphore()
        for dev in me.others + me.dev_z:
            pl.semaphore_signal(bar, 1, device_id=dev, device_id_type=MESH)
        k = 2
        lc = []
        for j, (off, w) in enumerate(GROUPS):
            for t in range(3):
                start(k, wqkv_s.at[:, pl.ds(t * D + off, w)], w_qkv[j].at[(*mine, slice(None), pl.ds(t * w, w))])
            lc.append((w_qkv[j], k))
            k += 1
        for src, dst in [(wout_s, w_out), (wdn_s, w_dn)] + [(wup_s.at[:, pl.ds(j * fc, fc)], w_up[j]) for j in range(CHUNKS)]:
            start(k, src, dst.at[mine])
            lc.append((dst, k))
            k += 1
        late[12] = jnp.zeros((16, 128), F32)
        for i, r in enumerate(vec_in):
            late[12, i : i + 1, 0 : r.shape[0]] = r[...].astype(F32).reshape(1, r.shape[0])
        up_row = lax.broadcasted_iota(jnp.int32, (16, 128), 0) == UPB
        given = late[12]
        small[mine] = jnp.where(
            up_row, pltpu.roll(given, me.c * 64, 1), pltpu.roll(given, (me.own * 2 + me.c) * 16, 1)).astype(BF)

        arrived = []
        n_x = 0
        nodes = x.g + [x.out, x.dn] + x.u + [x.sm]
        for i, (node, buf) in enumerate(zip(nodes, [*w_qkv, w_out, w_dn, *w_up, small])):
            is_small = node is x.sm
            gz = GatherZ(me, buf, (sem_out, (4 if is_small else 0,)), (sem_z, (i,)))

            def zgo(i=i, gz=gz):
                if i < len(lc):
                    wait_for((lc[i][0], mine), (local, (lc[i][1],)))
                gz.go()

            node.zgo = zgo
            for j, part in enumerate(x.d if node is x.dn else [node]):
                gt = Gather(me, buf, [(sem_out, (k,)) for k in ((5, 6) if is_small else (0, 1))], (sem_x, (n_x,)), part in direct_of(x),
                            pl.ds(j, 1) if node is x.dn else ALL)
                n_x += 1

                def first(gt=gt, gz=gz):
                    if gz not in arrived:
                        arrived.append(gz)
                        gz.wait()
                    gt.xy()

                part.xy, part.turn, part.core, part.ready = first, gt.turn, gt.core, gt.ready

        def scatter(node, i, buf, four, zs=ALL):
            sc = Scatter(me, buf, four, ((sem_out, (2,)), (sem_out, (3,))), (sem_s, (i,)), node in direct_of(x), zs)
            node.core, node.xy, node.turn = sc.core, sc.xy, sc.turn
            return sc

        for i, (node, b) in enumerate(zip(x.sq + [x.so] + x.su, [*g_qkv, g_wout, *g_up])):
            sc = scatter(node, i, b, rs_bufs[i])
            node.last = ScatterZ(me, sc.s2, rzs[i], (sem_out, (3,)), (sem_sz, (i,)))

            def total(sc=sc, node=node):
                sc.sum()
                node.last.go()

            node.sum = total
        x.dw.last = ScatterZ(me, s2_dn, rzs[-1], (sem_out, (3,)), (sem_sz, (n_groups + 1 + CHUNKS,)))
        summed = []
        for j, node in enumerate(x.sd):
            sc = scatter(node, n_groups + 1 + CHUNKS + j, g_dn, (*dn_bufs[j], s2_dn), pl.ds(j, 1))

            def total(sc=sc):
                sc.sum()
                summed.append(0)
                if len(summed) == CHUNKS:
                    x.dw.last.go()

            node.sum = total

        def r_qkv(j):
            off, w = GROUPS[j]
            res = x.sq[j].last.result()
            for t in range(3):
                gqkv_o[:, t * D + off : t * D + off + w] = res[:, t * w : (t + 1) * w]

        def r_up(j):
            gup_o[:, j * fc : (j + 1) * fc] = x.su[j].last.result()

        def r_dn():
            gdn_o[...] = x.dw.last.result()

        def r_out():
            gout_o[...] = x.so.last.result()

        te, tl = Total(me, early, sem_e), Total(me, late, sem_l)

        def te_go():
            for i, r in enumerate(EARLY):
                for q in range(4):
                    early[0, 4 * i + q : 4 * i + q + 1, :] = sg[r : r + 1, q * 128 : (q + 1) * 128]
            for q in range(4):
                for w in range(4):
                    early[0, 16 + 4 * q + w : 17 + 4 * q + w, :] = sg[12 + q : 13 + q, w * 128 : (w + 1) * 128]
            te.go()

        def tl_go():
            for i, r in enumerate(LATE):
                for q in range(4):
                    late[0, 4 * i + q : 4 * i + q + 1, :] = sg[r : r + 1, q * 128 : (q + 1) * 128]
            tl.go()

        shift = lax.rem(128 - (me.own * 2 + me.c) * 16, 128)

        def r_early():
            e = te.result()
            early[12] = pltpu.roll(e, shift, 1)
            early[13] = pltpu.roll(e, lax.rem(128 - me.c * 64, 128), 1)
            for i, r in enumerate(EARLY):
                sg_o[r : r + 1, :] = early[12, pl.ds(4 * i + me.z, 1), :]
            upb_o[...] = early[13, pl.ds(16 + 4 * me.z + me.own, 1), :]

        def r_late():
            late[12] = pltpu.roll(tl.result(), shift, 1)
            for i, r in enumerate(LATE):
                sg_o[r : r + 1, :] = late[12, pl.ds(4 * i + me.z, 1), :]

        x.te.go, x.te.turn, x.te.end = te_go, te.turn, r_early
        x.tl.go, x.tl.turn, x.tl.end = tl_go, tl.turn, r_late
        x.dw.end, x.so.end = r_dn, r_out
        for j in range(n_groups):
            x.sq[j].end = functools.partial(r_qkv, j)
        for j in range(CHUNKS):
            x.su[j].end = functools.partial(r_up, j)
        pl.semaphore_wait(bar, 10)
    else:
        lc = [start(2 + i, w_in[i], b) for i, b in enumerate(w_qkv + [w_out, w_dn] + w_up)]
    t_ = plan(x)
    now(t_.start)

    kk = lax.broadcasted_iota(jnp.int32, (slots, slots), 0)
    qq = lax.broadcasted_iota(jnp.int32, (slots, slots), 1)

    def masks(r):
        across = jnp.broadcast_to(ord_ref[pl.ds(r, 1), :].astype(F32), (slots, slots))
        down = across.T
        ok = jnp.logical_or(jnp.logical_and(kk < len_ref[r], down <= across), kk == qq)
        bias[r] = jnp.where(ok, 0.0, MASKED)

    rows_loop(masks)
    sg[...] = jnp.zeros_like(sg)
    cx.wait()

    def v(i):
        return vec[i : i + 1, :]

    def add(i, val):
        sg[i : i + 1, :] += val

    def col(val):
        return jnp.sum(val, axis=0, keepdims=True)

    def norm(val):
        centred = val - jnp.mean(val, axis=-1, keepdims=True)
        spread = jnp.mean(centred * centred, axis=-1, keepdims=True)
        r = lax.rsqrt(spread + EPS)
        return centred * r, r

    now(t_.pre)
    if comm:
        for zz in range(4):
            tot = None
            for w in range(4):
                for q in range(2):
                    b = small[zz, w, q].astype(F32)
                    tot = b if tot is None else tot + b
            vec[0:16, zz * 128 : (zz + 1) * 128] = tot
            for w in range(4):
                two = (small[zz, w, 0].astype(F32) + small[zz, w, 1].astype(F32))[UPB : UPB + 1]
                vec[16 + zz : 17 + zz, w * 128 : (w + 1) * 128] = two
    else:
        vec[0:16] = vec_in[...]
        vec[16:20] = upb_in[...]

    def first_norm(r):
        t = tok(r)
        n, _ = norm(xv[t].astype(F32))
        h = (n * v(LN1G) + v(LN1B)).astype(BF)
        h1[t] = h
        h1t[:, t] = h.T

    rows_loop(first_norm, unroll=2)
    lane = lax.broadcasted_iota(jnp.int32, (slots, 128), 1)
    first_half = lane < HEAD_DIM

    def heads_apart(pair):
        nil = jnp.zeros_like(pair)
        return jnp.where(first_half, pair, nil), jnp.where(first_half, nil, pair)

    now(t_.proj)
    shifts, mults = [], []
    for j, (off, w) in enumerate(GROUPS):
        if not comm:
            lc[j].wait()
        shifts.append(
            jnp.concatenate([v(QB)[:, off : off + w], jnp.zeros((1, w), F32), v(VB)[:, off : off + w]], axis=1))
        mults.append(jnp.where(lax.broadcasted_iota(jnp.int32, (1, 3 * w), 1) < w, SCALE, 1.0))

    def attend(r):
        t = tok(r)
        for j, (off, w) in enumerate(GROUPS):
            proj = ((nn(h1[t], w_qkv[j][...].reshape(D, 3 * w)) + shifts[j]) * mults[j]).astype(BF)
            qkv[j][t] = proj
            for p in range(w // 128):
                q = proj[:, p * 128 : (p + 1) * 128]
                k = proj[:, w + p * 128 : w + (p + 1) * 128]
                u = proj[:, 2 * w + p * 128 : 2 * w + (p + 1) * 128]
                sc = nt(jnp.concatenate(heads_apart(k), axis=0), q)
                ps = []
                for h in range(2):
                    sh = sc[h * slots : (h + 1) * slots] + bias[r]
                    e = jnp.exp(sh - jnp.max(sh, axis=0, keepdims=True))
                    ps.append((e * (1.0 / jnp.sum(e, axis=0, keepdims=True))).astype(BF))
                probs = jnp.concatenate(ps, axis=0)
                pt[r, off // 128 + p] = probs
                m = tn(probs, jnp.concatenate(heads_apart(u), axis=0))
                mixed[t, pl.ds(off + p * 128, 128)] = m.astype(BF)

    rows_loop(attend, t_.attend, unroll=2)
    cg.wait()
    if not comm:
        lc[n_groups].wait()

    def second_norm(r):
        t = tok(r)
        x1 = xv[t].astype(F32) + (nn(mixed[t], w_out[...].reshape(D, D)) + v(OB))
        n, rr = norm(x1)
        h = (n * v(LN2G) + v(LN2B)).astype(BF)
        h2[t] = h
        h2t[:, t] = h.T
        n2[t] = n
        r2[t] = jnp.broadcast_to(rr, (slots, 128))
        x1v[t] = x1
        add(DB, col(gv[t].astype(F32)))

    rows_loop(second_norm, t_.second_norm, unroll=2)
    if not comm:
        lc[n_groups + 1].wait()

    for j in range(CHUNKS):
        if not comm:
            lc[n_groups + 2 + j].wait()
        ub = vec[16 + j : 17 + j, :]

        def feed(r, j=j, ub=ub):
            t = tok(r)
            wu = w_up[j][...].reshape(D, fc)
            wd = w_dn[j].reshape(fc, D)
            pre = nn(h2[t], wu) + ub
            sq_ = pre * pre
            c1 = 0.5 + 0.5 * jnp.tanh(pre * (GELU_A + GELU_B * sq_))
            a = pre * c1
            slope = c1 + a * ((1.0 - c1) * (2.0 * GELU_A + 6.0 * GELU_B * sq_))
            dpre = nt(gv[t], wd) * slope
            dl = dpre.astype(BF)
            act[pl.ds(pl.multiple_of(j * tokens + r * slots, slots), slots)] = a.astype(BF)
            dpre_s[pl.ds(pl.multiple_of((j % 2) * tokens + r * slots, slots), slots)] = dl
            add(12 + j, col(dpre))
            back = nt(dl, wu)
            dh2[t] = back if j == 0 else dh2[t] + back

        def grads(i, j=j - 1):
            cut = pl.ds(pl.multiple_of(i * (fc // 2), fc // 2), fc // 2)
            g = tn(act[j * tokens : (j + 1) * tokens, cut], gv[...])
            g_dn[j, pl.ds(2 * i, 2)] = g.astype(BF).reshape(2, *g_dn.shape[2:])
            cut = pl.ds(pl.multiple_of(i * (D // 2), D // 2), D // 2)
            g = nn(h2t[cut], dpre_s[(j % 2) * tokens : (j % 2 + 1) * tokens])
            g_up[j][pl.ds(2 * i, 2)] = g.astype(BF).reshape(2, *g_up[j].shape[1:])

        rows_loop(feed, t_.feed[j], unroll=2, also=grads if j else None)
        now(t_.fed[j])
    j = CHUNKS - 1
    now(t_.gdn)
    g_dn[j] = tn(act[j * tokens : (j + 1) * tokens], gv[...]).astype(BF).reshape(g_dn.shape[1:])
    now(t_.gup)
    g_up[j][...] = nn(h2t[...], dpre_s[(j % 2) * tokens : (j % 2 + 1) * tokens]).astype(BF).reshape(g_up[j].shape)

    def second_back(r):
        t = tok(r)
        g2 = dh2[t]
        n = n2[t]
        add(LN2G, col(g2 * n))
        add(LN2B, col(g2))
        e = g2 * v(LN2G)
        dx = gv[t].astype(F32) + r2[t, pl.ds(0, 1)] * (
            e - jnp.mean(e, axis=-1, keepdims=True) - n * jnp.mean(e * n, axis=-1, keepdims=True))
        dx1[t] = dx
        add(OB, col(dx))
        da[t] = dx.astype(BF)

    rows_loop(second_back, t_.second_back, unroll=2)
    now(t_.gwout)
    g_wout[...] = tn(mixed[...], da[...]).astype(BF).reshape(g_wout.shape)

    for j in reversed(range(n_groups)):
        off, w = GROUPS[j]

        def back(r, j=j, off=off, w=w):
            t = tok(r)
            wo_ = w_out[...].reshape(D, D)[off : off + w]
            dmix = nt(da[t], wo_).astype(BF)
            for p in range(w // 128):
                q = qkv[j][t, pl.ds(p * 128, 128)]
                k = qkv[j][t, pl.ds(w + p * 128, 128)]
                u = qkv[j][t, pl.ds(2 * w + p * 128, 128)]
                dm = dmix[:, p * 128 : (p + 1) * 128]
                probs = pt[r, off // 128 + p]
                dm0, dm1 = heads_apart(dm)
                q0, q1 = heads_apart(q)
                dv = nn(probs[:slots], dm0) + nn(probs[slots:], dm1)
                dpt = nt(jnp.concatenate(heads_apart(u), axis=0), dm)
                ds = []
                for h in range(2):
                    pf = probs[h * slots : (h + 1) * slots].astype(F32)
                    d = dpt[h * slots : (h + 1) * slots]
                    ds.append((pf * (d - jnp.sum(pf * d, axis=0, keepdims=True))).astype(BF))
                dk = nn(ds[0], q0) + nn(ds[1], q1)
                dq = tn(jnp.concatenate(ds, axis=0), jnp.concatenate(heads_apart(k), axis=0)) * SCALE
                s0 = off + p * 128
                sg[QB : QB + 1, s0 : s0 + 128] += col(dq)
                sg[VB : VB + 1, s0 : s0 + 128] += col(dv)
                dproj[j][t, pl.ds(p * 128, 128)] = dq.astype(BF)
                dproj[j][t, pl.ds(w + p * 128, 128)] = dk.astype(BF)
                dproj[j][t, pl.ds(2 * w + p * 128, 128)] = dv.astype(BF)

        rows_loop(back, t_.back[j], unroll=2)
        now(t_.gqkv[j])
        g_qkv[j][...] = nn(h1t[...], dproj[j][...]).astype(BF).reshape(g_qkv[j].shape)

    def first_back(r):
        t = tok(r)
        g1 = None
        for j, (off, w) in enumerate(GROUPS):
            part = nt(dproj[j][t], w_qkv[j][...].reshape(D, 3 * w))
            g1 = part if g1 is None else g1 + part
        n, rr = norm(xv[t].astype(F32))
        add(LN1G, col(g1 * n))
        add(LN1B, col(g1))
        e = g1 * v(LN1G)
        dx1[t] = dx1[t] + rr * (e - jnp.mean(e, axis=-1, keepdims=True) - n * jnp.mean(e * n, axis=-1, keepdims=True))
        y = x1v[t] + v(DB)
        for j in range(CHUNKS):
            y = y + nn(act[pl.ds(pl.multiple_of(j * tokens + r * slots, slots), slots)], w_dn[j].reshape(fc, D))
        outv[t] = y.astype(BF)

    rows_loop(first_back, t_.first_back, unroll=2)
    ci = start(1, dx1, ig_hbm)
    co = start(0, outv, out_hbm)
    now(t_.tail)
    if comm:
        for k in range(4):
            room = me.bytes[id(sem_out), k] // (D * 2)
            wait_for((act, (pl.ds(0, room),)), (sem_out, (k,)))
        wait_for((small, (THREE, 0, 0)), (sem_out, (4,)))
        wait_for((small, (ALL, THREE, 0)), (sem_out, (5,)))
        wait_for((small, (ALL, FOUR, 0)), (sem_out, (6,)))
        te.finish()
        tl.finish()
    else:
        sg_o[...] = sg[...]
        out_c = [start(2 + i, b, o) for i, (b, o) in enumerate(zip(g_qkv + [g_wout, g_dn] + g_up, g_out))]
        for cp in out_c:
            cp.wait()
    co.wait()
    ci.wait()


def run_layer(comm, rows, slots, ff, operands):
    tokens = rows * slots
    fc = ff // CHUNKS
    n_groups = len(GROUPS)
    blk = lambda r, c: (4, 4, 2, r, c)
    pieces = [blk(D // 32, 3 * w) for _, w in GROUPS] + [blk(D // 32, D), blk(ff // 32, D)] + [blk(D // 32, fc)] * CHUNKS
    any_ = pl.BlockSpec(memory_space=pl.ANY)
    vm = pl.BlockSpec(memory_space=pltpu.VMEM)
    smem = pl.BlockSpec(memory_space=pltpu.SMEM)
    in_specs = [any_, any_, smem, vm] + [vm] * (9 if comm else 1)
    out_shape = [jax.ShapeDtypeStruct((tokens, D), BF), jax.ShapeDtypeStruct((tokens, D), F32)]
    out_specs = [any_, any_]
    if comm:
        in_specs += [any_] * 4
        out_shape += [jax.ShapeDtypeStruct(s, F32) for s in (
            (D // 32, 3 * D), (D // 32, D), (D // 32, ff), (ff // 32, D), (8, 128), (1, 128))]
        out_specs += [vm] * 6
    else:
        in_specs += [any_] * len(pieces) + [vm]
        out_shape += [jax.ShapeDtypeStruct(s, BF) for s in pieces] + [jax.ShapeDtypeStruct((16, D), F32)]
        out_specs += [any_] * len(pieces) + [vm]
    V = pltpu.VMEM
    scratch = [
        V((tokens, D), BF), V((tokens, D), BF), V((rows, slots, slots), F32), V((tokens, D), BF), V((D, tokens), BF),
        V((rows, D // 128, 2 * slots, slots), BF), V((tokens, D), BF), V((tokens, D), F32), V((tokens, 128), F32),
        V((tokens, D), BF), V((D, tokens), BF), V((tokens, D), F32), V((tokens, D), F32), V((tokens, D), F32),
        V((CHUNKS * tokens, fc), BF), V((2 * tokens, fc), BF), V((tokens, D), BF), V((tokens, D), BF), V((24, D), F32), V((16, D), F32),
    ]
    scratch += [V((tokens, 3 * w), BF) for _, w in GROUPS] * 2
    scratch += [V(s, BF) for s in pieces] * 2
    scratch += [pltpu.SemaphoreType.DMA((2 + len(pieces),))]
    if comm:
        dma = pltpu.SemaphoreType.DMA
        n_xy = n_groups + 1 + 2 * CHUNKS
        n_z = len(pieces) + 1
        scratch += [V(blk(16, 128), BF), V((14, 32, 128), F32), V((13, 16, 128), F32)]
        scratch += [dma((7,)), dma((n_z,)), dma((n_xy + 1, 3)), dma((n_xy, 3)), dma((n_z,)), dma((4,)), dma((4,))]
        whole = pieces[: n_groups + 1] + pieces[n_groups + 2 :]
        by_way = lambda straight, z, r, c: V((z, r, c) if straight else (2, z, r, c // 2), BF)
        straight = scatter_direct(n_groups)
        for i, s in enumerate(whole):
            r, c = s[3:]
            scratch += [V((4, 4, r, c), BF), by_way(i in straight, 4, r, c), V((2, 4, r, c), BF), V((4, r, c), BF)]
        r, c = pieces[n_groups + 1][3:]
        for j in range(CHUNKS):
            scratch += [V((1, 4, r, c), BF), by_way(len(whole) + j in straight, 1, r, c), V((2, 1, r, c), BF)]
        scratch += [V((4, r, c), BF)]
        scratch += [V((3, *s[3:]), BF) for s in whole] + [V((3, r, c), BF)]
    return pl.pallas_call(
        functools.partial(layer, comm, rows, slots, ff),
        out_shape=out_shape, in_specs=in_specs, out_specs=out_specs, scratch_shapes=scratch,
        compiler_params=pltpu.CompilerParams(
            vmem_limit_bytes=63 << 20, **(dict(collective_id=0, has_side_effects=True) if comm else {})),
        cost_estimate=pl.CostEstimate(flops=22_000_000_000, bytes_accessed=6 << 20, transcendentals=4 << 20),
    )(*operands)


def deliver(n, *refs):
    ins, outs, bufs, sems = refs[: n + 2], refs[n + 2 : n + 2 + n + 9], refs[n + 2 + n + 9 : -1], refs[-1]
    parts = []
    for i in range(n):
        rows = ins[i].shape[0]
        step = min(rows, 256)
        parts += [(i, pl.ds(k, step)) for k in range(0, rows, step)]
    first = [pltpu.make_async_copy(ins[i].at[s], bufs[i].at[s], sems.at[0, k]) for k, (i, s) in enumerate(parts)]
    second = [pltpu.make_async_copy(bufs[i].at[s], outs[i].at[s], sems.at[1, k]) for k, (i, s) in enumerate(parts)]
    for cp in first:
        cp.start()
    for i in range(9):
        o = outs[n + i]
        k = o.shape[0]
        o[...] = (ins[n][i : i + 1, 0:k] if i < 8 else ins[n + 1][:, 0:k]).reshape(k)
    for a, b in zip(first, second):
        a.wait()
        b.start()
    for cp in second:
        cp.wait()


def run_deliver(share, up_share, results):
    n = len(results) - 2
    any_ = pl.BlockSpec(memory_space=pl.ANY)
    vm = pl.BlockSpec(memory_space=pltpu.VMEM)
    n_parts = sum(max(1, r.shape[0] // 256) for r in results[:n])
    return pl.pallas_call(
        functools.partial(deliver, n),
        out_shape=[jax.ShapeDtypeStruct(r.shape, r.dtype) for r in results[:n]]
        + [jax.ShapeDtypeStruct((share,), F32)] * 8 + [jax.ShapeDtypeStruct((up_share,), F32)],
        in_specs=[any_] * n + [vm, vm], out_specs=[any_] * n + [vm] * 9,
        scratch_shapes=[pltpu.VMEM(r.shape, r.dtype) for r in results[:n]] + [pltpu.SemaphoreType.DMA((2, n_parts))],
        compiler_params=pltpu.CompilerParams(vmem_limit_bytes=63 << 20),
    )(*results)


def shards(
    inputs, lengths, slot_order, ln1_gain, ln1_bias, w_qkv, q_bias, v_bias, w_out, out_bias, ln2_gain, ln2_bias, w_up, up_bias,
    w_down, down_bias, cotangent, fast=True,
):
    rows, slots, width = inputs.shape
    tokens = rows * slots
    ff = w_up.shape[1]
    flat = (inputs.reshape(tokens, width), cotangent.reshape(tokens, width), lengths, slot_order)
    vectors = [ln1_gain, ln1_bias, q_bias, v_bias, out_bias, ln2_gain, ln2_bias, down_bias, up_bias]
    axes = ("dp", "shard")
    if fast:
        res = run_layer(True, rows, slots, ff, flat + (*vectors, w_qkv, w_out, w_up, w_down))
        out, ig, gqkv, gout, gup, gdn, *mine, upb = run_deliver(ln1_gain.shape[0], up_bias.shape[0], res)
    else:
        full = lambda a: lax.all_gather(a, axes, axis=0, tiled=True)
        whole = [full(a).astype(F32) for a in vectors]
        packed = jnp.stack(whole[:8] + [jnp.zeros((width,), F32)] * 8)
        wq, wo, wu, wd = full(w_qkv), full(w_out), full(w_up), full(w_down)
        fc = ff // CHUNKS
        cut = lambda a: a.reshape(4, 4, 2, a.shape[0] // 32, a.shape[1])
        pieces = [cut(jnp.concatenate([wq[:, t * D + off : t * D + off + w] for t in range(3)], axis=1)) for off, w in GROUPS]
        pieces += [cut(wo), cut(wd)] + [cut(wu[:, j * fc : (j + 1) * fc]) for j in range(CHUNKS)]
        res = run_layer(False, rows, slots, ff, flat + (packed, *pieces, whole[8].reshape(CHUNKS, fc)))
        out, ig, sg = res[0], res[1], res[-1]
        back = [r.astype(F32).reshape(-1, r.shape[-1]) for r in res[2:-1]]
        own = lambda a: lax.psum_scatter(a, axes, scatter_dimension=0, tiled=True)
        k = len(GROUPS)
        gq = jnp.concatenate([back[j][:, t * w : (t + 1) * w] for t in range(3) for j, (_, w) in enumerate(GROUPS)], axis=1)
        gqkv, gout, gdn, gup = own(gq), own(back[k]), own(back[k + 1]), own(jnp.concatenate(back[k + 2 :], axis=1))
        mine = own(sg[0:8].T).T
        upb = own(sg[12:16].reshape(-1))
    shape = (rows, slots, width)
    return (
        out.reshape(shape), ig.reshape(shape), mine[LN1G], mine[LN1B], gqkv, mine[QB], mine[VB], gout, mine[OB], mine[LN2G],
        mine[LN2B], gup, upb, gdn, mine[DB],
    )


def solution(mesh):
    whole = P(("dp", "shard"))
    fast = mesh.shape["dp"] == 8 and mesh.shape["shard"] == 4
    return jax.shard_map(
        functools.partial(shards, fast=fast), mesh=mesh, in_specs=(whole,) * 17, out_specs=(whole,) * 15, check_vma=False)
```

```python
import functools
import types

import jax
import jax.numpy as jnp
from jax import lax
from jax.experimental import pallas as pl
from jax.experimental.pallas import tpu as pltpu
from jax.sharding import PartitionSpec as P

HEADS = 8
HEAD_DIM = 64
SCALE = HEAD_DIM ** (-0.5)
EPS = 1e-05
MASKED = -1e30
GELU_A = 0.7978845608028654
GELU_B = GELU_A * 0.044715
MESH = pl.DeviceIdType.MESH
BF = jnp.bfloat16
F32 = jnp.float32

D = HEADS * HEAD_DIM
GROUPS = ((0, 256), (256, 256))
CHUNKS = 4
LN1G, LN1B, QB, VB, OB, LN2G, LN2B, DB, UPB = range(9)
LATE = (LN1G, LN1B, QB, VB)
EARLY = (OB, LN2G, LN2B, DB)


def nn(a, b):
    return lax.dot_general(a, b, (((1,), (0,)), ((), ())), preferred_element_type=F32)


def nt(a, b):
    return lax.dot_general(a, b, (((1,), (1,)), ((), ())), preferred_element_type=F32)


def tn(a, b):
    return lax.dot_general(a, b, (((0,), (0,)), ((), ())), preferred_element_type=F32)


def nothing():
    pass


class Node:
    def __getattr__(self, name):
        return nothing


def plan(x):
    return types.SimpleNamespace(
        start=(x.sm.zgo, x.g[0].zgo, x.g[1].zgo, x.out.zgo, x.u[0].zgo, x.dn.zgo, x.u[1].zgo, x.u[2].zgo, x.u[3].zgo,),
        pre=(x.sm.xy, x.g[0].xy, x.sm.turn, x.sm.core, x.sm.ready,),
        proj=((x.g[1].xy, x.out.xy, x.g[0].turn, x.u[0].xy, x.g[0].core, x.g[0].ready,), (x.u[0].turn, x.d[1].xy, x.g[1].core, x.g[1].ready,)),
        attend=({1: (x.g[1].turn, x.d[0].xy, x.out.turn, x.u[1].xy,)}, {1: (x.out.core, x.d[0].turn, x.u[2].xy,)}),
        second_norm={0: (x.out.ready, x.u[0].core, x.u[1].turn, x.d[1].turn, x.d[2].xy, x.u[3].xy,), 1: (x.d[0].core,)},
        feed=(
            {0: (x.u[0].ready, x.d[0].ready, x.u[2].turn, x.d[3].xy,), 1: (x.u[1].core, x.d[1].core,)},
            {0: (x.u[1].ready, x.d[1].ready,), 1: (x.u[2].core, x.u[3].turn,)},
            {0: (x.u[2].ready, x.d[2].ready,), 1: (x.u[3].core, x.sd[0].xy, x.su[0].xy, x.d[3].core,)},
            {0: (x.u[3].ready, x.d[3].ready,), 1: (x.sd[0].turn, x.sd[1].xy,)},
        ),
        fed=((x.d[2].turn,), (x.d[2].core, x.d[3].turn, x.sd[0].core, x.su[0].core,), (x.sd[1].core, x.su[1].core,), (x.su[0].turn, x.su[1].xy, x.sd[2].core, x.su[2].core,)),
        gdn=(),
        gup=(x.sd[0].sum, x.sd[3].core,),
        second_back={0: (x.sd[1].turn, x.sd[2].xy, x.su[3].core,), 1: (x.su[2].xy,)},
        gwout=(x.te.go, x.su[0].sum, x.su[1].turn, x.sd[3].xy, x.su[3].xy,),
        back=({0: (x.su[3].turn, x.sq[1].core, x.te.end,), 1: (x.sd[2].sum, x.su[2].sum, x.so.turn, x.sq[1].xy,)}, {0: (x.so.core,), 1: (x.sd[1].sum, x.sd[2].turn, x.su[2].turn, x.so.xy, x.te.turn,)}),
        gqkv=((x.sd[3].sum, x.su[3].sum, x.su[1].end,), (x.su[1].sum, x.sd[3].turn, x.su[0].end,)),
        first_back={0: (x.so.sum, x.sq[0].core,), 1: (x.sq[0].xy, x.su[2].end,)},
        tail=(x.tl.go, x.sq[1].sum, x.tl.turn, x.sq[0].sum, x.su[3].end, x.dw.end, x.so.end, x.sq[1].end, x.tl.end, x.sq[0].end,),
    )


def direct_of(x):
    return (x.sm, x.g[0], x.sq[0], x.sq[1],)


def scatter_direct(n_groups):
    return (0, 1,)


class Place:
    def __init__(self):
        dp, sh = lax.axis_index("dp"), lax.axis_index("shard")
        self.z, x, y, self.c = lax.div(dp, 2), lax.rem(dp, 2), lax.div(sh, 2), lax.rem(sh, 2)
        nx, ny, self.nc = 1 - x, 1 - y, 1 - self.c
        self.own, self.ix, self.iy, self.id = x * 2 + y, nx * 2 + y, x * 2 + ny, nx * 2 + ny
        self.zs = [lax.rem(self.z + k, 4) for k in (1, 2, 3)]
        at = lambda z, x, y, c: (z * 2 + x, y * 2 + c)
        self.dev_z = [at(k, x, y, self.c) for k in self.zs]
        self.dev_x, self.dev_y = at(self.z, nx, y, self.c), at(self.z, x, ny, self.c)
        self.dev_d, self.dev_c = at(self.z, nx, ny, self.c), at(self.z, x, y, self.nc)
        self.others = [self.dev_x, self.dev_y, self.dev_d, self.dev_c, at(self.z, nx, y, self.nc), at(self.z, x, ny, self.nc),
                       at(self.z, nx, ny, self.nc)]
        self.bytes = {}

    def send(self, src, dst, out, land, device):
        at = lambda pair: pair[0].at[pair[1]]
        cp = pltpu.make_async_remote_copy(
            src_ref=at(src), dst_ref=at(dst), send_sem=at(out), recv_sem=at(land), device_id=device, device_id_type=MESH)
        cp.start()
        n = 1
        for k in cp.src_ref.shape:
            n *= k
        key = (id(out[0]), *out[1])
        self.bytes[key] = self.bytes.get(key, 0) + n * jnp.dtype(cp.src_ref.dtype).itemsize


ALL = slice(None)
TWO, THREE, FOUR = pl.ds(0, 2), pl.ds(0, 3), pl.ds(0, 4)


def wait_for(like, sem):
    ref = like[0].at[like[1]]
    pltpu.make_async_copy(ref, ref, sem[0].at[sem[1]]).wait()


class GatherZ:
    def __init__(self, me, buf, out, land):
        self.me, self.buf, self.out, self.land = me, buf, out, land

    def go(self):
        me = self.me
        own = (self.buf, (me.z, me.own, me.c))
        for k in range(3):
            me.send(own, own, self.out, self.land, me.dev_z[k])

    def wait(self):
        wait_for((self.buf, (THREE, 0, 0)), self.land)


class Gather:
    def __init__(self, me, buf, outs, land, direct=False, zs=ALL):
        self.me, self.buf, self.direct, self.zs = me, buf, direct, zs
        self.out, self.out_core = outs
        self.land = [(land[0], (*land[1], k)) for k in range(3)]

    def line(self, i, cols=None):
        return self.buf, (self.zs, i, self.me.c) + (() if cols is None else (ALL, cols))

    def to(self, line, k, device):
        self.me.send(line, line, self.out_core if k == 2 else self.out, self.land[k], device)

    def xy(self):
        me, own = self.me, self.line(self.me.own)
        self.to(own, 0, me.dev_x)
        self.to(own, 0, me.dev_y)
        if self.direct:
            self.to(own, 1, me.dev_d)
        self.to(own, 2, me.dev_c)

    def turn(self):
        me = self.me
        wait_for((self.buf, (self.zs, TWO, 0)), self.land[0])
        if not self.direct:
            h = self.buf.shape[-1] // 2
            self.to(self.line(me.ix, pl.ds(0, h)), 1, me.dev_y)
            self.to(self.line(me.iy, pl.ds(h, h)), 1, me.dev_x)
        self.to(self.line(me.ix), 2, me.dev_c)
        self.to(self.line(me.iy), 2, me.dev_c)

    def core(self):
        wait_for((self.buf, (self.zs, 0, 0)), self.land[1])
        self.to(self.line(self.me.id), 2, self.me.dev_c)

    def ready(self):
        wait_for((self.buf, (self.zs, FOUR, 0)), self.land[2])


class Scatter:
    def __init__(self, me, buf, bufs, outs, land, direct=False, zs=ALL):
        self.me, self.buf, self.direct, self.zs = me, buf, direct, zs
        self.out_core, self.out = outs
        self.rc, self.r1, self.r2, self.s2 = bufs
        self.land = [(land[0], (*land[1], k)) for k in range(3)]
        self.h = buf.shape[-1] // 2

    def core(self):
        me = self.me
        me.send((self.buf, (self.zs, ALL, me.nc)), (self.rc, (ALL,)), self.out_core, self.land[0], me.dev_c)

    def to(self, where, cols, dst, k, device):
        me = self.me
        me.send((self.rc, (ALL, where) + (() if cols is None else (ALL, cols))), dst, self.out, self.land[k], device)

    def xy(self):
        me, h, rc, r1, r2 = self.me, self.h, self.rc, self.r1, self.r2
        wait_for((rc, (ALL,)), self.land[0])
        first = 0 if self.zs == ALL else self.zs.start
        for i in range(rc.shape[0]):
            rc[i] = rc[i] + self.buf[first + i, :, me.c]
        if self.direct:
            self.to(me.ix, None, (r2, (0,)), 2, me.dev_x)
            self.to(me.iy, None, (r2, (1,)), 2, me.dev_y)
            self.to(me.id, None, (r1, (ALL,)), 2, me.dev_d)
        else:
            lo, hi = pl.ds(0, h), pl.ds(h, h)
            self.to(me.id, lo, (r1, (0,)), 1, me.dev_x)
            self.to(me.id, hi, (r1, (1,)), 1, me.dev_y)
            self.to(me.ix, lo, (r2, (0, ALL, ALL, lo)), 2, me.dev_x)
            self.to(me.iy, hi, (r2, (1, ALL, ALL, hi)), 2, me.dev_y)

    def turn(self):
        me, h, rc, r1, r2 = self.me, self.h, self.rc, self.r1, self.r2
        wait_for((r1, (ALL,)), self.land[1])
        rc[:, me.iy, :, :h] = rc[:, me.iy, :, :h] + r1[0]
        rc[:, me.ix, :, h:] = rc[:, me.ix, :, h:] + r1[1]
        lo, hi = pl.ds(0, h), pl.ds(h, h)
        self.to(me.iy, lo, (r2, (1, ALL, ALL, lo)), 2, me.dev_y)
        self.to(me.ix, hi, (r2, (0, ALL, ALL, hi)), 2, me.dev_x)

    def sum(self):
        f = lambda v: v.astype(F32)
        if self.direct:
            wait_for((self.rc, (ALL, THREE)), self.land[2])
        else:
            wait_for((self.r2, (ALL,)), self.land[2])
        tot = f(self.rc[:, self.me.own]) + (f(self.r2[0]) + f(self.r2[1]))
        if self.direct:
            tot = tot + f(self.r1[...])
        self.s2[self.zs] = tot.astype(BF)


class ScatterZ:
    def __init__(self, me, s2, rz, out, land):
        self.me, self.s2, self.rz, self.out, self.land = me, s2, rz, out, land

    def go(self):
        me = self.me
        for k in range(3):
            me.send((self.s2, (me.zs[k],)), (self.rz, (k,)), self.out, self.land, me.dev_z[k])

    def result(self):
        wait_for((self.rz, (ALL,)), self.land)
        f = lambda v: v.astype(F32)
        return (f(self.s2[self.me.z]) + f(self.rz[0])) + (f(self.rz[1]) + f(self.rz[2]))


class Total:
    def __init__(self, me, buf, sems):
        self.me, self.buf = me, buf
        self.sem = [(sems, (k,)) for k in range(4)]

    def go(self):
        for i, d in enumerate(self.me.others):
            self.me.send((self.buf, (0,)), (self.buf, (2 + i,)), self.sem[0], self.sem[1], d)

    def turn(self):
        me, b = self.me, self.buf
        wait_for((b, (pl.ds(2, 7),)), self.sem[1])
        b[1] = ((b[0] + b[2]) + (b[3] + b[4])) + ((b[5] + b[6]) + (b[7] + b[8]))
        for k in range(3):
            me.send((b, (1,)), (b, (9 + k,)), self.sem[2], self.sem[3], me.dev_z[k])

    def result(self):
        b = self.buf
        wait_for((b, (pl.ds(9, 3),)), self.sem[3])
        return (b[1] + b[9]) + (b[10] + b[11])

    def finish(self):
        wait_for((self.buf, (pl.ds(2, 7),)), self.sem[0])
        wait_for((self.buf, (pl.ds(9, 3),)), self.sem[2])


def layer(comm, rows, slots, ff, *refs):
    tokens = rows * slots
    fc = ff // CHUNKS
    it = iter(refs)
    take = lambda n: [next(it) for _ in range(n)]
    n_groups = len(GROUPS)
    n_pieces = n_groups + 2 + CHUNKS
    x_hbm, g_hbm, len_ref, ord_ref = take(4)
    if comm:
        vec_in = take(9)
        wqkv_s, wout_s, wup_s, wdn_s = take(4)
    else:
        vec_in, = take(1)
        w_in = take(n_pieces)
        upb_in, = take(1)
    out_hbm, ig_hbm = take(2)
    if comm:
        gqkv_o, gout_o, gup_o, gdn_o, sg_o, upb_o = take(6)
    else:
        g_out = take(n_pieces)
        sg_o, = take(1)
    xv, gv, bias, h1, h1t, pt, mixed, n2, r2, h2, h2t, x1v, dx1, dh2, act, dpre_s, da, outv, vec, sg = take(20)
    qkv = take(n_groups)
    dproj = take(n_groups)
    w_qkv = take(n_groups)
    w_out, w_dn = take(2)
    w_up = take(CHUNKS)
    g_qkv = take(n_groups)
    g_wout, g_dn = take(2)
    g_up = take(CHUNKS)
    local, = take(1)
    x = types.SimpleNamespace(
        sm=Node(), g=[Node() for _ in GROUPS], out=Node(), dn=Node(), u=[Node() for _ in range(CHUNKS)], d=[Node() for _ in range(CHUNKS)],
        sq=[Node() for _ in GROUPS], so=Node(), su=[Node() for _ in range(CHUNKS)], sd=[Node() for _ in range(CHUNKS)], dw=Node(),
        te=Node(), tl=Node())

    def tok(r):
        return pl.ds(pl.multiple_of(r * slots, slots), slots)

    def now(todo):
        for f in todo:
            f()

    def rows_loop(body, ticks={}, unroll=1, also=None):
        def step(i, carry):
            if comm:
                for k in ticks:

                    @pl.when(i == k)
                    def _(k=k):
                        now(ticks[k])

            for u in range(unroll):
                body(i * unroll + u)
            if also is not None:
                also(i)
            return carry

        lax.fori_loop(0, rows // unroll, step, 0)

    def start(slot, src, dst):
        cp = pltpu.make_async_copy(src, dst, local.at[slot])
        cp.start()
        return cp

    cx = start(0, x_hbm, xv)
    cg = start(1, g_hbm, gv)
    if comm:
        small, early, late, sem_out, sem_z, sem_x, sem_s, sem_sz, sem_e, sem_l = take(10)
        rs_bufs = [take(4) for _ in range(n_groups + 1 + CHUNKS)]
        dn_bufs = [take(3) for _ in range(CHUNKS)]
        s2_dn, = take(1)
        rzs = take(n_groups + 2 + CHUNKS)
        me = Place()
        mine = (me.z, me.own, me.c)
        bar = pltpu.get_barrier_semaphore()
        for dev in me.others + me.dev_z:
            pl.semaphore_signal(bar, 1, device_id=dev, device_id_type=MESH)
        k = 2
        lc = []
        for j, (off, w) in enumerate(GROUPS):
            for t in range(3):
                start(k, wqkv_s.at[:, pl.ds(t * D + off, w)], w_qkv[j].at[(*mine, slice(None), pl.ds(t * w, w))])
            lc.append((w_qkv[j], k))
            k += 1
        for src, dst in [(wout_s, w_out), (wdn_s, w_dn)] + [(wup_s.at[:, pl.ds(j * fc, fc)], w_up[j]) for j in range(CHUNKS)]:
            start(k, src, dst.at[mine])
            lc.append((dst, k))
            k += 1
        late[12] = jnp.zeros((16, 128), F32)
        for i, r in enumerate(vec_in):
            late[12, i : i + 1, 0 : r.shape[0]] = r[...].astype(F32).reshape(1, r.shape[0])
        up_row = lax.broadcasted_iota(jnp.int32, (16, 128), 0) == UPB
        given = late[12]
        small[mine] = jnp.where(
            up_row, pltpu.roll(given, me.c * 64, 1), pltpu.roll(given, (me.own * 2 + me.c) * 16, 1)).astype(BF)

        arrived = []
        n_x = 0
        nodes = x.g + [x.out, x.dn] + x.u + [x.sm]
        for i, (node, buf) in enumerate(zip(nodes, [*w_qkv, w_out, w_dn, *w_up, small])):
            is_small = node is x.sm
            gz = GatherZ(me, buf, (sem_out, (4 if is_small else 0,)), (sem_z, (i,)))

            def zgo(i=i, gz=gz):
                if i < len(lc):
                    wait_for((lc[i][0], mine), (local, (lc[i][1],)))
                gz.go()

            node.zgo = zgo
            for j, part in enumerate(x.d if node is x.dn else [node]):
                gt = Gather(me, buf, [(sem_out, (k,)) for k in ((5, 6) if is_small else (0, 1))], (sem_x, (n_x,)), part in direct_of(x),
                            pl.ds(j, 1) if node is x.dn else ALL)
                n_x += 1

                def first(gt=gt, gz=gz):
                    if gz not in arrived:
                        arrived.append(gz)
                        gz.wait()
                    gt.xy()

                part.xy, part.turn, part.core, part.ready = first, gt.turn, gt.core, gt.ready

        def scatter(node, i, buf, four, zs=ALL):
            sc = Scatter(me, buf, four, ((sem_out, (2,)), (sem_out, (3,))), (sem_s, (i,)), node in direct_of(x), zs)
            node.core, node.xy, node.turn = sc.core, sc.xy, sc.turn
            return sc

        for i, (node, b) in enumerate(zip(x.sq + [x.so] + x.su, [*g_qkv, g_wout, *g_up])):
            sc = scatter(node, i, b, rs_bufs[i])
            node.last = ScatterZ(me, sc.s2, rzs[i], (sem_out, (3,)), (sem_sz, (i,)))

            def total(sc=sc, node=node):
                sc.sum()
                node.last.go()

            node.sum = total
        x.dw.last = ScatterZ(me, s2_dn, rzs[-1], (sem_out, (3,)), (sem_sz, (n_groups + 1 + CHUNKS,)))
        summed = []
        for j, node in enumerate(x.sd):
            sc = scatter(node, n_groups + 1 + CHUNKS + j, g_dn, (*dn_bufs[j], s2_dn), pl.ds(j, 1))

            def total(sc=sc):
                sc.sum()
                summed.append(0)
                if len(summed) == CHUNKS:
                    x.dw.last.go()

            node.sum = total

        def r_qkv(j):
            off, w = GROUPS[j]
            res = x.sq[j].last.result()
            for t in range(3):
                gqkv_o[:, t * D + off : t * D + off + w] = res[:, t * w : (t + 1) * w]

        def r_up(j):
            gup_o[:, j * fc : (j + 1) * fc] = x.su[j].last.result()

        def r_dn():
            gdn_o[...] = x.dw.last.result()

        def r_out():
            gout_o[...] = x.so.last.result()

        te, tl = Total(me, early, sem_e), Total(me, late, sem_l)

        def te_go():
            for i, r in enumerate(EARLY):
                for q in range(4):
                    early[0, 4 * i + q : 4 * i + q + 1, :] = sg[r : r + 1, q * 128 : (q + 1) * 128]
            for q in range(4):
                for w in range(4):
                    early[0, 16 + 4 * q + w : 17 + 4 * q + w, :] = sg[12 + q : 13 + q, w * 128 : (w + 1) * 128]
            te.go()

        def tl_go():
            for i, r in enumerate(LATE):
                for q in range(4):
                    late[0, 4 * i + q : 4 * i + q + 1, :] = sg[r : r + 1, q * 128 : (q + 1) * 128]
            tl.go()

        shift = lax.rem(128 - (me.own * 2 + me.c) * 16, 128)

        def r_early():
            e = te.result()
            early[12] = pltpu.roll(e, shift, 1)
            early[13] = pltpu.roll(e, lax.rem(128 - me.c * 64, 128), 1)
            for i, r in enumerate(EARLY):
                sg_o[r : r + 1, :] = early[12, pl.ds(4 * i + me.z, 1), :]
            upb_o[...] = early[13, pl.ds(16 + 4 * me.z + me.own, 1), :]

        def r_late():
            late[12] = pltpu.roll(tl.result(), shift, 1)
            for i, r in enumerate(LATE):
                sg_o[r : r + 1, :] = late[12, pl.ds(4 * i + me.z, 1), :]

        x.te.go, x.te.turn, x.te.end = te_go, te.turn, r_early
        x.tl.go, x.tl.turn, x.tl.end = tl_go, tl.turn, r_late
        x.dw.end, x.so.end = r_dn, r_out
        for j in range(n_groups):
            x.sq[j].end = functools.partial(r_qkv, j)
        for j in range(CHUNKS):
            x.su[j].end = functools.partial(r_up, j)
        pl.semaphore_wait(bar, 10)
    else:
        lc = [start(2 + i, w_in[i], b) for i, b in enumerate(w_qkv + [w_out, w_dn] + w_up)]
    t_ = plan(x)
    now(t_.start)

    kk = lax.broadcasted_iota(jnp.int32, (slots, slots), 0)
    qq = lax.broadcasted_iota(jnp.int32, (slots, slots), 1)

    def masks(r):
        across = jnp.broadcast_to(ord_ref[pl.ds(r, 1), :].astype(F32), (slots, slots))
        down = across.T
        ok = jnp.logical_or(jnp.logical_and(kk < len_ref[r], down <= across), kk == qq)
        bias[r] = jnp.where(ok, 0.0, MASKED)

    rows_loop(masks)
    sg[...] = jnp.zeros_like(sg)
    cx.wait()

    def v(i):
        return vec[i : i + 1, :]

    def add(i, val):
        sg[i : i + 1, :] += val

    def col(val):
        return jnp.sum(val, axis=0, keepdims=True)

    def norm(val):
        centred = val - jnp.mean(val, axis=-1, keepdims=True)
        spread = jnp.mean(centred * centred, axis=-1, keepdims=True)
        r = lax.rsqrt(spread + EPS)
        return centred * r, r

    now(t_.pre)
    if comm:
        for zz in range(4):
            tot = None
            for w in range(4):
                for q in range(2):
                    b = small[zz, w, q].astype(F32)
                    tot = b if tot is None else tot + b
            vec[0:16, zz * 128 : (zz + 1) * 128] = tot
            for w in range(4):
                two = (small[zz, w, 0].astype(F32) + small[zz, w, 1].astype(F32))[UPB : UPB + 1]
                vec[16 + zz : 17 + zz, w * 128 : (w + 1) * 128] = two
    else:
        vec[0:16] = vec_in[...]
        vec[16:20] = upb_in[...]

    def first_norm(r):
        t = tok(r)
        n, _ = norm(xv[t].astype(F32))
        h = (n * v(LN1G) + v(LN1B)).astype(BF)
        h1[t] = h
        h1t[:, t] = h.T

    rows_loop(first_norm, unroll=2)
    lane = lax.broadcasted_iota(jnp.int32, (slots, 128), 1)
    first_half = lane < HEAD_DIM

    def heads_apart(pair):
        nil = jnp.zeros_like(pair)
        return jnp.where(first_half, pair, nil), jnp.where(first_half, nil, pair)

    for j, (off, w) in enumerate(GROUPS):
        now(t_.proj[j])
        if not comm:
            lc[j].wait()
        shift_ = jnp.concatenate([v(QB)[:, off : off + w], jnp.zeros((1, w), F32), v(VB)[:, off : off + w]], axis=1)
        mult = jnp.where(lax.broadcasted_iota(jnp.int32, (1, 3 * w), 1) < w, SCALE, 1.0)

        def attend(r, j=j, off=off, w=w, shift_=shift_, mult=mult):
            t = tok(r)
            proj = ((nn(h1[t], w_qkv[j][...].reshape(D, 3 * w)) + shift_) * mult).astype(BF)
            qkv[j][t] = proj
            for p in range(w // 128):
                q = proj[:, p * 128 : (p + 1) * 128]
                k = proj[:, w + p * 128 : w + (p + 1) * 128]
                u = proj[:, 2 * w + p * 128 : 2 * w + (p + 1) * 128]
                sc = nt(jnp.concatenate(heads_apart(k), axis=0), q)
                ps = []
                for h in range(2):
                    sh = sc[h * slots : (h + 1) * slots] + bias[r]
                    e = jnp.exp(sh - jnp.max(sh, axis=0, keepdims=True))
                    ps.append((e * (1.0 / jnp.sum(e, axis=0, keepdims=True))).astype(BF))
                probs = jnp.concatenate(ps, axis=0)
                pt[r, off // 128 + p] = probs
                m = tn(probs, jnp.concatenate(heads_apart(u), axis=0))
                mixed[t, pl.ds(off + p * 128, 128)] = m.astype(BF)

        rows_loop(attend, t_.attend[j], unroll=2)
    cg.wait()
    if not comm:
        lc[n_groups].wait()

    def second_norm(r):
        t = tok(r)
        x1 = xv[t].astype(F32) + (nn(mixed[t], w_out[...].reshape(D, D)) + v(OB))
        n, rr = norm(x1)
        h = (n * v(LN2G) + v(LN2B)).astype(BF)
        h2[t] = h
        h2t[:, t] = h.T
        n2[t] = n
        r2[t] = jnp.broadcast_to(rr, (slots, 128))
        x1v[t] = x1
        add(DB, col(gv[t].astype(F32)))

    rows_loop(second_norm, t_.second_norm, unroll=2)
    if not comm:
        lc[n_groups + 1].wait()

    for j in range(CHUNKS):
        if not comm:
            lc[n_groups + 2 + j].wait()
        ub = vec[16 + j : 17 + j, :]

        def feed(r, j=j, ub=ub):
            t = tok(r)
            wu = w_up[j][...].reshape(D, fc)
            wd = w_dn[j].reshape(fc, D)
            pre = nn(h2[t], wu) + ub
            sq_ = pre * pre
            c1 = 0.5 + 0.5 * jnp.tanh(pre * (GELU_A + GELU_B * sq_))
            a = pre * c1
            slope = c1 + a * ((1.0 - c1) * (2.0 * GELU_A + 6.0 * GELU_B * sq_))
            dpre = nt(gv[t], wd) * slope
            dl = dpre.astype(BF)
            act[pl.ds(pl.multiple_of(j * tokens + r * slots, slots), slots)] = a.astype(BF)
            dpre_s[pl.ds(pl.multiple_of((j % 2) * tokens + r * slots, slots), slots)] = dl
            add(12 + j, col(dpre))
            back = nt(dl, wu)
            dh2[t] = back if j == 0 else dh2[t] + back

        def grads(i, j=j - 1):
            cut = pl.ds(pl.multiple_of(i * (fc // 2), fc // 2), fc // 2)
            g = tn(act[j * tokens : (j + 1) * tokens, cut], gv[...])
            g_dn[j, pl.ds(2 * i, 2)] = g.astype(BF).reshape(2, *g_dn.shape[2:])
            cut = pl.ds(pl.multiple_of(i * (D // 2), D // 2), D // 2)
            g = nn(h2t[cut], dpre_s[(j % 2) * tokens : (j % 2 + 1) * tokens])
            g_up[j][pl.ds(2 * i, 2)] = g.astype(BF).reshape(2, *g_up[j].shape[1:])

        rows_loop(feed, t_.feed[j], unroll=2, also=grads if j else None)
        now(t_.fed[j])
    j = CHUNKS - 1
    now(t_.gdn)
    g_dn[j] = tn(act[j * tokens : (j + 1) * tokens], gv[...]).astype(BF).reshape(g_dn.shape[1:])
    now(t_.gup)
    g_up[j][...] = nn(h2t[...], dpre_s[(j % 2) * tokens : (j % 2 + 1) * tokens]).astype(BF).reshape(g_up[j].shape)

    def second_back(r):
        t = tok(r)
        g2 = dh2[t]
        n = n2[t]
        add(LN2G, col(g2 * n))
        add(LN2B, col(g2))
        e = g2 * v(LN2G)
        dx = gv[t].astype(F32) + r2[t, pl.ds(0, 1)] * (
            e - jnp.mean(e, axis=-1, keepdims=True) - n * jnp.mean(e * n, axis=-1, keepdims=True))
        dx1[t] = dx
        add(OB, col(dx))
        da[t] = dx.astype(BF)

    rows_loop(second_back, t_.second_back, unroll=2)
    now(t_.gwout)
    g_wout[...] = tn(mixed[...], da[...]).astype(BF).reshape(g_wout.shape)

    for j in reversed(range(n_groups)):
        off, w = GROUPS[j]

        def back(r, j=j, off=off, w=w):
            t = tok(r)
            wo_ = w_out[...].reshape(D, D)[off : off + w]
            dmix = nt(da[t], wo_).astype(BF)
            for p in range(w // 128):
                q = qkv[j][t, pl.ds(p * 128, 128)]
                k = qkv[j][t, pl.ds(w + p * 128, 128)]
                u = qkv[j][t, pl.ds(2 * w + p * 128, 128)]
                dm = dmix[:, p * 128 : (p + 1) * 128]
                probs = pt[r, off // 128 + p]
                dm0, dm1 = heads_apart(dm)
                q0, q1 = heads_apart(q)
                dv = nn(probs[:slots], dm0) + nn(probs[slots:], dm1)
                dpt = nt(jnp.concatenate(heads_apart(u), axis=0), dm)
                ds = []
                for h in range(2):
                    pf = probs[h * slots : (h + 1) * slots].astype(F32)
                    d = dpt[h * slots : (h + 1) * slots]
                    ds.append((pf * (d - jnp.sum(pf * d, axis=0, keepdims=True))).astype(BF))
                dk = nn(ds[0], q0) + nn(ds[1], q1)
                dq = tn(jnp.concatenate(ds, axis=0), jnp.concatenate(heads_apart(k), axis=0)) * SCALE
                s0 = off + p * 128
                sg[QB : QB + 1, s0 : s0 + 128] += col(dq)
                sg[VB : VB + 1, s0 : s0 + 128] += col(dv)
                dproj[j][t, pl.ds(p * 128, 128)] = dq.astype(BF)
                dproj[j][t, pl.ds(w + p * 128, 128)] = dk.astype(BF)
                dproj[j][t, pl.ds(2 * w + p * 128, 128)] = dv.astype(BF)

        rows_loop(back, t_.back[j], unroll=2)
        now(t_.gqkv[j])
        g_qkv[j][...] = nn(h1t[...], dproj[j][...]).astype(BF).reshape(g_qkv[j].shape)

    def first_back(r):
        t = tok(r)
        g1 = None
        for j, (off, w) in enumerate(GROUPS):
            part = nt(dproj[j][t], w_qkv[j][...].reshape(D, 3 * w))
            g1 = part if g1 is None else g1 + part
        n, rr = norm(xv[t].astype(F32))
        add(LN1G, col(g1 * n))
        add(LN1B, col(g1))
        e = g1 * v(LN1G)
        dx1[t] = dx1[t] + rr * (e - jnp.mean(e, axis=-1, keepdims=True) - n * jnp.mean(e * n, axis=-1, keepdims=True))
        y = x1v[t] + v(DB)
        for j in range(CHUNKS):
            y = y + nn(act[pl.ds(pl.multiple_of(j * tokens + r * slots, slots), slots)], w_dn[j].reshape(fc, D))
        outv[t] = y.astype(BF)

    rows_loop(first_back, t_.first_back, unroll=2)
    ci = start(1, dx1, ig_hbm)
    co = start(0, outv, out_hbm)
    now(t_.tail)
    if comm:
        for k in range(4):
            room = me.bytes[id(sem_out), k] // (D * 2)
            wait_for((act, (pl.ds(0, room),)), (sem_out, (k,)))
        wait_for((small, (THREE, 0, 0)), (sem_out, (4,)))
        wait_for((small, (ALL, THREE, 0)), (sem_out, (5,)))
        wait_for((small, (ALL, FOUR, 0)), (sem_out, (6,)))
        te.finish()
        tl.finish()
    else:
        sg_o[...] = sg[...]
        out_c = [start(2 + i, b, o) for i, (b, o) in enumerate(zip(g_qkv + [g_wout, g_dn] + g_up, g_out))]
        for cp in out_c:
            cp.wait()
    co.wait()
    ci.wait()


def run_layer(comm, rows, slots, ff, operands):
    tokens = rows * slots
    fc = ff // CHUNKS
    n_groups = len(GROUPS)
    blk = lambda r, c: (4, 4, 2, r, c)
    pieces = [blk(D // 32, 3 * w) for _, w in GROUPS] + [blk(D // 32, D), blk(ff // 32, D)] + [blk(D // 32, fc)] * CHUNKS
    any_ = pl.BlockSpec(memory_space=pl.ANY)
    vm = pl.BlockSpec(memory_space=pltpu.VMEM)
    smem = pl.BlockSpec(memory_space=pltpu.SMEM)
    in_specs = [any_, any_, smem, vm] + [vm] * (9 if comm else 1)
    out_shape = [jax.ShapeDtypeStruct((tokens, D), BF), jax.ShapeDtypeStruct((tokens, D), F32)]
    out_specs = [any_, any_]
    if comm:
        in_specs += [any_] * 4
        out_shape += [jax.ShapeDtypeStruct(s, F32) for s in (
            (D // 32, 3 * D), (D // 32, D), (D // 32, ff), (ff // 32, D), (8, 128), (1, 128))]
        out_specs += [vm] * 6
    else:
        in_specs += [any_] * len(pieces) + [vm]
        out_shape += [jax.ShapeDtypeStruct(s, BF) for s in pieces] + [jax.ShapeDtypeStruct((16, D), F32)]
        out_specs += [any_] * len(pieces) + [vm]
    V = pltpu.VMEM
    scratch = [
        V((tokens, D), BF), V((tokens, D), BF), V((rows, slots, slots), F32), V((tokens, D), BF), V((D, tokens), BF),
        V((rows, D // 128, 2 * slots, slots), BF), V((tokens, D), BF), V((tokens, D), F32), V((tokens, 128), F32),
        V((tokens, D), BF), V((D, tokens), BF), V((tokens, D), F32), V((tokens, D), F32), V((tokens, D), F32),
        V((CHUNKS * tokens, fc), BF), V((2 * tokens, fc), BF), V((tokens, D), BF), V((tokens, D), BF), V((24, D), F32), V((16, D), F32),
    ]
    scratch += [V((tokens, 3 * w), BF) for _, w in GROUPS] * 2
    scratch += [V(s, BF) for s in pieces] * 2
    scratch += [pltpu.SemaphoreType.DMA((2 + len(pieces),))]
    if comm:
        dma = pltpu.SemaphoreType.DMA
        n_xy = n_groups + 1 + 2 * CHUNKS
        n_z = len(pieces) + 1
        scratch += [V(blk(16, 128), BF), V((14, 32, 128), F32), V((13, 16, 128), F32)]
        scratch += [dma((7,)), dma((n_z,)), dma((n_xy + 1, 3)), dma((n_xy, 3)), dma((n_z,)), dma((4,)), dma((4,))]
        whole = pieces[: n_groups + 1] + pieces[n_groups + 2 :]
        by_way = lambda straight, z, r, c: V((z, r, c) if straight else (2, z, r, c // 2), BF)
        straight = scatter_direct(n_groups)
        for i, s in enumerate(whole):
            r, c = s[3:]
            scratch += [V((4, 4, r, c), BF), by_way(i in straight, 4, r, c), V((2, 4, r, c), BF), V((4, r, c), BF)]
        r, c = pieces[n_groups + 1][3:]
        for j in range(CHUNKS):
            scratch += [V((1, 4, r, c), BF), by_way(len(whole) + j in straight, 1, r, c), V((2, 1, r, c), BF)]
        scratch += [V((4, r, c), BF)]
        scratch += [V((3, *s[3:]), BF) for s in whole] + [V((3, r, c), BF)]
    return pl.pallas_call(
        functools.partial(layer, comm, rows, slots, ff),
        out_shape=out_shape, in_specs=in_specs, out_specs=out_specs, scratch_shapes=scratch,
        compiler_params=pltpu.CompilerParams(
            vmem_limit_bytes=63 << 20, **(dict(collective_id=0, has_side_effects=True) if comm else {})),
        cost_estimate=pl.CostEstimate(flops=22_000_000_000, bytes_accessed=6 << 20, transcendentals=4 << 20),
    )(*operands)


def deliver(n, *refs):
    ins, outs, bufs, sems = refs[: n + 2], refs[n + 2 : n + 2 + n + 9], refs[n + 2 + n + 9 : -1], refs[-1]
    parts = []
    for i in range(n):
        rows = ins[i].shape[0]
        step = min(rows, 256)
        parts += [(i, pl.ds(k, step)) for k in range(0, rows, step)]
    first = [pltpu.make_async_copy(ins[i].at[s], bufs[i].at[s], sems.at[0, k]) for k, (i, s) in enumerate(parts)]
    second = [pltpu.make_async_copy(bufs[i].at[s], outs[i].at[s], sems.at[1, k]) for k, (i, s) in enumerate(parts)]
    for cp in first:
        cp.start()
    for i in range(9):
        o = outs[n + i]
        k = o.shape[0]
        o[...] = (ins[n][i : i + 1, 0:k] if i < 8 else ins[n + 1][:, 0:k]).reshape(k)
    for a, b in zip(first, second):
        a.wait()
        b.start()
    for cp in second:
        cp.wait()


def run_deliver(share, up_share, results):
    n = len(results) - 2
    any_ = pl.BlockSpec(memory_space=pl.ANY)
    vm = pl.BlockSpec(memory_space=pltpu.VMEM)
    n_parts = sum(max(1, r.shape[0] // 256) for r in results[:n])
    return pl.pallas_call(
        functools.partial(deliver, n),
        out_shape=[jax.ShapeDtypeStruct(r.shape, r.dtype) for r in results[:n]]
        + [jax.ShapeDtypeStruct((share,), F32)] * 8 + [jax.ShapeDtypeStruct((up_share,), F32)],
        in_specs=[any_] * n + [vm, vm], out_specs=[any_] * n + [vm] * 9,
        scratch_shapes=[pltpu.VMEM(r.shape, r.dtype) for r in results[:n]] + [pltpu.SemaphoreType.DMA((2, n_parts))],
        compiler_params=pltpu.CompilerParams(vmem_limit_bytes=63 << 20),
    )(*results)


def shards(
    inputs, lengths, slot_order, ln1_gain, ln1_bias, w_qkv, q_bias, v_bias, w_out, out_bias, ln2_gain, ln2_bias, w_up, up_bias,
    w_down, down_bias, cotangent, fast=True,
):
    rows, slots, width = inputs.shape
    tokens = rows * slots
    ff = w_up.shape[1]
    flat = (inputs.reshape(tokens, width), cotangent.reshape(tokens, width), lengths, slot_order)
    vectors = [ln1_gain, ln1_bias, q_bias, v_bias, out_bias, ln2_gain, ln2_bias, down_bias, up_bias]
    axes = ("dp", "shard")
    if fast:
        res = run_layer(True, rows, slots, ff, flat + (*vectors, w_qkv, w_out, w_up, w_down))
        out, ig, gqkv, gout, gup, gdn, *mine, upb = run_deliver(ln1_gain.shape[0], up_bias.shape[0], res)
    else:
        full = lambda a: lax.all_gather(a, axes, axis=0, tiled=True)
        whole = [full(a).astype(F32) for a in vectors]
        packed = jnp.stack(whole[:8] + [jnp.zeros((width,), F32)] * 8)
        wq, wo, wu, wd = full(w_qkv), full(w_out), full(w_up), full(w_down)
        fc = ff // CHUNKS
        cut = lambda a: a.reshape(4, 4, 2, a.shape[0] // 32, a.shape[1])
        pieces = [cut(jnp.concatenate([wq[:, t * D + off : t * D + off + w] for t in range(3)], axis=1)) for off, w in GROUPS]
        pieces += [cut(wo), cut(wd)] + [cut(wu[:, j * fc : (j + 1) * fc]) for j in range(CHUNKS)]
        res = run_layer(False, rows, slots, ff, flat + (packed, *pieces, whole[8].reshape(CHUNKS, fc)))
        out, ig, sg = res[0], res[1], res[-1]
        back = [r.astype(F32).reshape(-1, r.shape[-1]) for r in res[2:-1]]
        own = lambda a: lax.psum_scatter(a, axes, scatter_dimension=0, tiled=True)
        k = len(GROUPS)
        gq = jnp.concatenate([back[j][:, t * w : (t + 1) * w] for t in range(3) for j, (_, w) in enumerate(GROUPS)], axis=1)
        gqkv, gout, gdn, gup = own(gq), own(back[k]), own(back[k + 1]), own(jnp.concatenate(back[k + 2 :], axis=1))
        mine = own(sg[0:8].T).T
        upb = own(sg[12:16].reshape(-1))
    shape = (rows, slots, width)
    return (
        out.reshape(shape), ig.reshape(shape), mine[LN1G], mine[LN1B], gqkv, mine[QB], mine[VB], gout, mine[OB], mine[LN2G],
        mine[LN2B], gup, upb, gdn, mine[DB],
    )


def solution(mesh):
    whole = P(("dp", "shard"))
    fast = mesh.shape["dp"] == 8 and mesh.shape["shard"] == 4
    return jax.shard_map(
        functools.partial(shards, fast=fast), mesh=mesh, in_specs=(whole,) * 17, out_specs=(whole,) * 15, check_vma=False)
```

```python
import functools
import types

import jax
import jax.numpy as jnp
from jax import lax
from jax.experimental import pallas as pl
from jax.experimental.pallas import tpu as pltpu
from jax.sharding import PartitionSpec as P

HEADS = 8
HEAD_DIM = 64
SCALE = HEAD_DIM ** (-0.5)
EPS = 1e-05
MASKED = -1e30
GELU_A = 0.7978845608028654
GELU_B = GELU_A * 0.044715
MESH = pl.DeviceIdType.MESH
BF = jnp.bfloat16
F32 = jnp.float32

D = HEADS * HEAD_DIM
GROUPS = ((0, 256), (256, 256))
CHUNKS = 4
LN1G, LN1B, QB, VB, OB, LN2G, LN2B, DB, UPB = range(9)
LATE = (LN1G, LN1B, QB, VB)
EARLY = (OB, LN2G, LN2B, DB)


def nn(a, b):
    return lax.dot_general(a, b, (((1,), (0,)), ((), ())), preferred_element_type=F32)


def nt(a, b):
    return lax.dot_general(a, b, (((1,), (1,)), ((), ())), preferred_element_type=F32)


def tn(a, b):
    return lax.dot_general(a, b, (((0,), (0,)), ((), ())), preferred_element_type=F32)


def nothing():
    pass


class Node:
    def __getattr__(self, name):
        return nothing


def plan(x):
    return types.SimpleNamespace(
        start=(x.sm.zgo, x.g[0].zgo, x.g[1].zgo, x.out.zgo, x.u[0].zgo, x.dn.zgo, x.u[1].zgo, x.u[2].zgo, x.u[3].zgo,),
        pre=(x.sm.xy, x.g[0].xy, x.sm.turn, x.sm.core, x.sm.ready,),
        proj=((x.g[1].xy, x.out.xy, x.g[0].turn, x.u[0].xy, x.g[0].core, x.g[0].ready,), (x.u[0].turn, x.d[1].xy, x.g[1].core, x.g[1].ready,)),
        attend=({1: (x.g[1].turn, x.d[0].xy, x.out.turn, x.u[1].xy,)}, {1: (x.out.core, x.d[0].turn, x.u[2].xy,)}),
        second_norm={0: (x.out.ready, x.u[0].core, x.u[1].turn, x.d[1].turn, x.d[2].xy, x.u[3].xy,), 1: (x.d[0].core,)},
        feed=(
            {0: (x.u[0].ready, x.d[0].ready, x.u[2].turn, x.d[3].xy,), 1: (x.u[1].core, x.d[1].core,)},
            {0: (x.u[1].ready, x.d[1].ready,), 1: (x.u[2].core, x.u[3].turn,)},
            {0: (x.u[2].ready, x.d[2].ready,), 1: (x.u[3].core, x.sd[0].xy, x.su[0].xy, x.d[3].core,)},
            {0: (x.u[3].ready, x.d[3].ready,), 1: (x.sd[0].turn, x.sd[1].xy,)},
        ),
        fed=((x.d[2].turn,), (x.d[2].core, x.d[3].turn, x.sd[0].core, x.su[0].core,), (x.sd[1].core, x.su[1].core,), (x.su[0].turn, x.su[1].xy, x.sd[2].core, x.su[2].core,)),
        second_back={1: (x.sd[0].sum,)},
        after=(x.te.go, x.sd[1].turn, x.sd[2].xy, x.su[2].xy, x.su[0].sum, x.sd[3].core, x.su[3].core,),
        back=({0: (x.su[1].sum, x.sd[3].turn, x.sq[1].core, x.te.end,), 1: (x.sd[2].sum, x.su[3].turn, x.so.xy, x.sq[1].xy,)}, {1: (x.sd[1].sum, x.su[1].turn, x.sd[3].xy, x.su[3].xy, x.te.turn,)}),
        gqkv=((x.su[2].sum, x.sd[3].sum,), (x.sd[2].turn, x.su[2].turn, x.so.core, x.su[0].end,)),
        first_back={0: (x.su[3].sum, x.so.turn, x.sq[0].core, x.su[1].end,), 1: (x.sq[0].xy,)},
        tail=(x.tl.go, x.sq[1].sum, x.so.sum, x.tl.turn, x.sq[0].sum, x.su[2].end, x.su[3].end, x.dw.end, x.so.end, x.sq[1].end, x.tl.end, x.sq[0].end,),
    )


def direct_of(x):
    return (x.sm, x.g[0], x.sq[0], x.sq[1],)


def scatter_direct(n_groups):
    return (0, 1,)


class Place:
    def __init__(self):
        dp, sh = lax.axis_index("dp"), lax.axis_index("shard")
        self.z, x, y, self.c = lax.div(dp, 2), lax.rem(dp, 2), lax.div(sh, 2), lax.rem(sh, 2)
        nx, ny, self.nc = 1 - x, 1 - y, 1 - self.c
        self.own, self.ix, self.iy, self.id = x * 2 + y, nx * 2 + y, x * 2 + ny, nx * 2 + ny
        self.zs = [lax.rem(self.z + k, 4) for k in (1, 2, 3)]
        at = lambda z, x, y, c: (z * 2 + x, y * 2 + c)
        self.dev_z = [at(k, x, y, self.c) for k in self.zs]
        self.dev_x, self.dev_y = at(self.z, nx, y, self.c), at(self.z, x, ny, self.c)
        self.dev_d, self.dev_c = at(self.z, nx, ny, self.c), at(self.z, x, y, self.nc)
        self.others = [self.dev_x, self.dev_y, self.dev_d, self.dev_c, at(self.z, nx, y, self.nc), at(self.z, x, ny, self.nc),
                       at(self.z, nx, ny, self.nc)]
        self.bytes = {}

    def send(self, src, dst, out, land, device):
        at = lambda pair: pair[0].at[pair[1]]
        cp = pltpu.make_async_remote_copy(
            src_ref=at(src), dst_ref=at(dst), send_sem=at(out), recv_sem=at(land), device_id=device, device_id_type=MESH)
        cp.start()
        n = 1
        for k in cp.src_ref.shape:
            n *= k
        key = (id(out[0]), *out[1])
        self.bytes[key] = self.bytes.get(key, 0) + n * jnp.dtype(cp.src_ref.dtype).itemsize


ALL = slice(None)
TWO, THREE, FOUR = pl.ds(0, 2), pl.ds(0, 3), pl.ds(0, 4)


def wait_for(like, sem):
    ref = like[0].at[like[1]]
    pltpu.make_async_copy(ref, ref, sem[0].at[sem[1]]).wait()


class GatherZ:
    def __init__(self, me, buf, out, land):
        self.me, self.buf, self.out, self.land = me, buf, out, land

    def go(self):
        me = self.me
        own = (self.buf, (me.z, me.own, me.c))
        for k in range(3):
            me.send(own, own, self.out, self.land, me.dev_z[k])

    def wait(self):
        wait_for((self.buf, (THREE, 0, 0)), self.land)


class Gather:
    def __init__(self, me, buf, outs, land, direct=False, zs=ALL):
        self.me, self.buf, self.direct, self.zs = me, buf, direct, zs
        self.out, self.out_core = outs
        self.land = [(land[0], (*land[1], k)) for k in range(3)]

    def line(self, i, cols=None):
        return self.buf, (self.zs, i, self.me.c) + (() if cols is None else (ALL, cols))

    def to(self, line, k, device):
        self.me.send(line, line, self.out_core if k == 2 else self.out, self.land[k], device)

    def xy(self):
        me, own = self.me, self.line(self.me.own)
        self.to(own, 0, me.dev_x)
        self.to(own, 0, me.dev_y)
        if self.direct:
            self.to(own, 1, me.dev_d)
        self.to(own, 2, me.dev_c)

    def turn(self):
        me = self.me
        wait_for((self.buf, (self.zs, TWO, 0)), self.land[0])
        if not self.direct:
            h = self.buf.shape[-1] // 2
            self.to(self.line(me.ix, pl.ds(0, h)), 1, me.dev_y)
            self.to(self.line(me.iy, pl.ds(h, h)), 1, me.dev_x)
        self.to(self.line(me.ix), 2, me.dev_c)
        self.to(self.line(me.iy), 2, me.dev_c)

    def core(self):
        wait_for((self.buf, (self.zs, 0, 0)), self.land[1])
        self.to(self.line(self.me.id), 2, self.me.dev_c)

    def ready(self):
        wait_for((self.buf, (self.zs, FOUR, 0)), self.land[2])


class Scatter:
    def __init__(self, me, buf, bufs, outs, land, direct=False, zs=ALL):
        self.me, self.buf, self.direct, self.zs = me, buf, direct, zs
        self.out_core, self.out = outs
        self.rc, self.r1, self.r2, self.s2 = bufs
        self.land = [(land[0], (*land[1], k)) for k in range(3)]
        self.h = buf.shape[-1] // 2

    def core(self):
        me = self.me
        me.send((self.buf, (self.zs, ALL, me.nc)), (self.rc, (ALL,)), self.out_core, self.land[0], me.dev_c)

    def to(self, where, cols, dst, k, device):
        me = self.me
        me.send((self.rc, (ALL, where) + (() if cols is None else (ALL, cols))), dst, self.out, self.land[k], device)

    def xy(self):
        me, h, rc, r1, r2 = self.me, self.h, self.rc, self.r1, self.r2
        wait_for((rc, (ALL,)), self.land[0])
        first = 0 if self.zs == ALL else self.zs.start
        for i in range(rc.shape[0]):
            rc[i] = rc[i] + self.buf[first + i, :, me.c]
        if self.direct:
            self.to(me.ix, None, (r2, (0,)), 2, me.dev_x)
            self.to(me.iy, None, (r2, (1,)), 2, me.dev_y)
            self.to(me.id, None, (r1, (ALL,)), 2, me.dev_d)
        else:
            lo, hi = pl.ds(0, h), pl.ds(h, h)
            self.to(me.id, lo, (r1, (0,)), 1, me.dev_x)
            self.to(me.id, hi, (r1, (1,)), 1, me.dev_y)
            self.to(me.ix, lo, (r2, (0, ALL, ALL, lo)), 2, me.dev_x)
            self.to(me.iy, hi, (r2, (1, ALL, ALL, hi)), 2, me.dev_y)

    def turn(self):
        me, h, rc, r1, r2 = self.me, self.h, self.rc, self.r1, self.r2
        wait_for((r1, (ALL,)), self.land[1])
        rc[:, me.iy, :, :h] = rc[:, me.iy, :, :h] + r1[0]
        rc[:, me.ix, :, h:] = rc[:, me.ix, :, h:] + r1[1]
        lo, hi = pl.ds(0, h), pl.ds(h, h)
        self.to(me.iy, lo, (r2, (1, ALL, ALL, lo)), 2, me.dev_y)
        self.to(me.ix, hi, (r2, (0, ALL, ALL, hi)), 2, me.dev_x)

    def sum(self):
        f = lambda v: v.astype(F32)
        if self.direct:
            wait_for((self.rc, (ALL, THREE)), self.land[2])
        else:
            wait_for((self.r2, (ALL,)), self.land[2])
        tot = f(self.rc[:, self.me.own]) + (f(self.r2[0]) + f(self.r2[1]))
        if self.direct:
            tot = tot + f(self.r1[...])
        self.s2[self.zs] = tot.astype(BF)


class ScatterZ:
    def __init__(self, me, s2, rz, out, land):
        self.me, self.s2, self.rz, self.out, self.land = me, s2, rz, out, land

    def go(self):
        me = self.me
        for k in range(3):
            me.send((self.s2, (me.zs[k],)), (self.rz, (k,)), self.out, self.land, me.dev_z[k])

    def result(self):
        wait_for((self.rz, (ALL,)), self.land)
        f = lambda v: v.astype(F32)
        return (f(self.s2[self.me.z]) + f(self.rz[0])) + (f(self.rz[1]) + f(self.rz[2]))


class Total:
    def __init__(self, me, buf, sems):
        self.me, self.buf = me, buf
        self.sem = [(sems, (k,)) for k in range(4)]

    def go(self):
        for i, d in enumerate(self.me.others):
            self.me.send((self.buf, (0,)), (self.buf, (2 + i,)), self.sem[0], self.sem[1], d)

    def turn(self):
        me, b = self.me, self.buf
        wait_for((b, (pl.ds(2, 7),)), self.sem[1])
        b[1] = ((b[0] + b[2]) + (b[3] + b[4])) + ((b[5] + b[6]) + (b[7] + b[8]))
        for k in range(3):
            me.send((b, (1,)), (b, (9 + k,)), self.sem[2], self.sem[3], me.dev_z[k])

    def result(self):
        b = self.buf
        wait_for((b, (pl.ds(9, 3),)), self.sem[3])
        return (b[1] + b[9]) + (b[10] + b[11])

    def finish(self):
        wait_for((self.buf, (pl.ds(2, 7),)), self.sem[0])
        wait_for((self.buf, (pl.ds(9, 3),)), self.sem[2])


def layer(comm, rows, slots, ff, *refs):
    tokens = rows * slots
    fc = ff // CHUNKS
    it = iter(refs)
    take = lambda n: [next(it) for _ in range(n)]
    n_groups = len(GROUPS)
    n_pieces = n_groups + 2 + CHUNKS
    x_hbm, g_hbm, len_hbm, ord_hbm = take(4)
    if comm:
        vec_hbm = take(9)
        wqkv_s, wout_s, wup_s, wdn_s = take(4)
    else:
        vec_in, = take(1)
        w_in = take(n_pieces)
        upb_in, = take(1)
    out_hbm, ig_hbm = take(2)
    if comm:
        results = take(6)
    else:
        g_out = take(n_pieces)
        sg_o, = take(1)
    xv, gv, bias, h1, h1t, pt, mixed, n2, r2, h2, h2t, x1v, dx1, dh2, act, dpre_s, da, outv, vec, sg, len_ref, ord_ref = take(22)
    qkv = take(n_groups)
    dproj = take(n_groups)
    w_qkv = take(n_groups)
    w_out, w_dn = take(2)
    w_up = take(CHUNKS)
    g_qkv = take(n_groups)
    g_wout, g_dn = take(2)
    g_up = take(CHUNKS)
    local, = take(1)
    x = types.SimpleNamespace(
        sm=Node(), g=[Node() for _ in GROUPS], out=Node(), dn=Node(), u=[Node() for _ in range(CHUNKS)], d=[Node() for _ in range(CHUNKS)],
        sq=[Node() for _ in GROUPS], so=Node(), su=[Node() for _ in range(CHUNKS)], sd=[Node() for _ in range(CHUNKS)], dw=Node(),
        te=Node(), tl=Node())

    def tok(r):
        return pl.ds(pl.multiple_of(r * slots, slots), slots)

    def now(todo):
        for f in todo:
            f()

    def rows_loop(body, ticks={}, unroll=1, also=None):
        def step(i, carry):
            if comm:
                for k in ticks:

                    @pl.when(i == k)
                    def _(k=k):
                        now(ticks[k])

            for u in range(unroll):
                body(i * unroll + u)
            if also is not None:
                also(i)
            return carry

        lax.fori_loop(0, rows // unroll, step, 0)

    def start(slot, src, dst):
        cp = pltpu.make_async_copy(src, dst, local.at[slot])
        cp.start()
        return cp

    cx = start(0, x_hbm, xv)
    cg = start(1, g_hbm, gv)
    n_l = 2 + n_pieces
    cl = [start(n_l, len_hbm, len_ref), start(n_l + 1, ord_hbm, ord_ref)]
    if comm:
        gqkv_o, gout_o, gup_o, gdn_o, sg_o, upb_o = held = take(6)
        vec_in = take(9)
        cv = [start(n_l + 2 + i, a, b) for i, (a, b) in enumerate(zip(vec_hbm, vec_in))]
        given_back = []

        def hand(i):
            given_back.append(start(n_l + 11 + i, held[i], results[i]))

        small, early, late, sem_out, sem_z, sem_x, sem_s, sem_sz, sem_e, sem_l = take(10)
        rs_bufs = [take(4) for _ in range(n_groups + 1 + CHUNKS)]
        dn_bufs = [take(3) for _ in range(CHUNKS)]
        s2_dn, = take(1)
        rzs = take(n_groups + 2 + CHUNKS)
        me = Place()
        mine = (me.z, me.own, me.c)
        bar = pltpu.get_barrier_semaphore()
        for dev in me.others + me.dev_z:
            pl.semaphore_signal(bar, 1, device_id=dev, device_id_type=MESH)
        k = 2
        lc = []
        for j, (off, w) in enumerate(GROUPS):
            for t in range(3):
                start(k, wqkv_s.at[:, pl.ds(t * D + off, w)], w_qkv[j].at[(*mine, slice(None), pl.ds(t * w, w))])
            lc.append((w_qkv[j], k))
            k += 1
        for src, dst in [(wout_s, w_out), (wdn_s, w_dn)] + [(wup_s.at[:, pl.ds(j * fc, fc)], w_up[j]) for j in range(CHUNKS)]:
            start(k, src, dst.at[mine])
            lc.append((dst, k))
            k += 1
        late[12] = jnp.zeros((16, 128), F32)
        for cp in cv:
            cp.wait()
        for i, r in enumerate(vec_in):
            late[12, i : i + 1, 0 : r.shape[0]] = r[...].astype(F32).reshape(1, r.shape[0])
        up_row = lax.broadcasted_iota(jnp.int32, (16, 128), 0) == UPB
        given = late[12]
        small[mine] = jnp.where(
            up_row, pltpu.roll(given, me.c * 64, 1), pltpu.roll(given, (me.own * 2 + me.c) * 16, 1)).astype(BF)

        arrived = []
        n_x = 0
        nodes = x.g + [x.out, x.dn] + x.u + [x.sm]
        for i, (node, buf) in enumerate(zip(nodes, [*w_qkv, w_out, w_dn, *w_up, small])):
            is_small = node is x.sm
            gz = GatherZ(me, buf, (sem_out, (4 if is_small else 0,)), (sem_z, (i,)))

            def zgo(i=i, gz=gz):
                if i < len(lc):
                    wait_for((lc[i][0], mine), (local, (lc[i][1],)))
                gz.go()

            node.zgo = zgo
            for j, part in enumerate(x.d if node is x.dn else [node]):
                gt = Gather(me, buf, [(sem_out, (k,)) for k in ((5, 6) if is_small else (0, 1))], (sem_x, (n_x,)), part in direct_of(x),
                            pl.ds(j, 1) if node is x.dn else ALL)
                n_x += 1

                def first(gt=gt, gz=gz):
                    if gz not in arrived:
                        arrived.append(gz)
                        gz.wait()
                    gt.xy()

                part.xy, part.turn, part.core, part.ready = first, gt.turn, gt.core, gt.ready

        def scatter(node, i, buf, four, zs=ALL):
            sc = Scatter(me, buf, four, ((sem_out, (2,)), (sem_out, (3,))), (sem_s, (i,)), node in direct_of(x), zs)
            node.core, node.xy, node.turn = sc.core, sc.xy, sc.turn
            return sc

        for i, (node, b) in enumerate(zip(x.sq + [x.so] + x.su, [*g_qkv, g_wout, *g_up])):
            sc = scatter(node, i, b, rs_bufs[i])
            node.last = ScatterZ(me, sc.s2, rzs[i], (sem_out, (3,)), (sem_sz, (i,)))

            def total(sc=sc, node=node):
                sc.sum()
                node.last.go()

            node.sum = total
        x.dw.last = ScatterZ(me, s2_dn, rzs[-1], (sem_out, (3,)), (sem_sz, (n_groups + 1 + CHUNKS,)))
        summed = []
        for j, node in enumerate(x.sd):
            sc = scatter(node, n_groups + 1 + CHUNKS + j, g_dn, (*dn_bufs[j], s2_dn), pl.ds(j, 1))

            def total(sc=sc):
                sc.sum()
                summed.append(0)
                if len(summed) == CHUNKS:
                    x.dw.last.go()

            node.sum = total

        def r_qkv(j):
            off, w = GROUPS[j]
            res = x.sq[j].last.result()
            for t in range(3):
                gqkv_o[:, t * D + off : t * D + off + w] = res[:, t * w : (t + 1) * w]

        def r_up(j):
            gup_o[:, j * fc : (j + 1) * fc] = x.su[j].last.result()

        def r_dn():
            gdn_o[...] = x.dw.last.result()

        def r_out():
            gout_o[...] = x.so.last.result()

        te, tl = Total(me, early, sem_e), Total(me, late, sem_l)

        def te_go():
            for i, r in enumerate(EARLY):
                for q in range(4):
                    early[0, 4 * i + q : 4 * i + q + 1, :] = sg[r : r + 1, q * 128 : (q + 1) * 128]
            for q in range(4):
                for w in range(4):
                    early[0, 16 + 4 * q + w : 17 + 4 * q + w, :] = sg[12 + q : 13 + q, w * 128 : (w + 1) * 128]
            te.go()

        def tl_go():
            for i, r in enumerate(LATE):
                for q in range(4):
                    late[0, 4 * i + q : 4 * i + q + 1, :] = sg[r : r + 1, q * 128 : (q + 1) * 128]
            tl.go()

        shift = lax.rem(128 - (me.own * 2 + me.c) * 16, 128)

        def r_early():
            e = te.result()
            early[12] = pltpu.roll(e, shift, 1)
            early[13] = pltpu.roll(e, lax.rem(128 - me.c * 64, 128), 1)
            for i, r in enumerate(EARLY):
                sg_o[r : r + 1, :] = early[12, pl.ds(4 * i + me.z, 1), :]
            upb_o[...] = early[13, pl.ds(16 + 4 * me.z + me.own, 1), :]

        def r_late():
            late[12] = pltpu.roll(tl.result(), shift, 1)
            for i, r in enumerate(LATE):
                sg_o[r : r + 1, :] = late[12, pl.ds(4 * i + me.z, 1), :]

        x.te.go, x.te.turn, x.te.end = te_go, te.turn, r_early
        x.tl.go, x.tl.turn, x.tl.end = tl_go, tl.turn, r_late
        x.dw.end, x.so.end = r_dn, r_out
        for j in range(n_groups):
            x.sq[j].end = functools.partial(r_qkv, j)
        for j in range(CHUNKS):
            x.su[j].end = functools.partial(r_up, j)
        pl.semaphore_wait(bar, 10)
    else:
        lc = [start(2 + i, w_in[i], b) for i, b in enumerate(w_qkv + [w_out, w_dn] + w_up)]
    t_ = plan(x)
    now(t_.start)

    kk = lax.broadcasted_iota(jnp.int32, (slots, slots), 0)
    qq = lax.broadcasted_iota(jnp.int32, (slots, slots), 1)

    def masks(r):
        across = jnp.broadcast_to(ord_ref[pl.ds(r, 1), :].astype(F32), (slots, slots))
        down = across.T
        ok = jnp.logical_or(jnp.logical_and(kk < len_ref[r], down <= across), kk == qq)
        bias[r] = jnp.where(ok, 0.0, MASKED)

    for cp in cl:
        cp.wait()
    rows_loop(masks)
    sg[...] = jnp.zeros_like(sg)
    cx.wait()

    def v(i):
        return vec[i : i + 1, :]

    def add(i, val):
        sg[i : i + 1, :] += val

    def col(val):
        return jnp.sum(val, axis=0, keepdims=True)

    def norm(val):
        centred = val - jnp.mean(val, axis=-1, keepdims=True)
        spread = jnp.mean(centred * centred, axis=-1, keepdims=True)
        r = lax.rsqrt(spread + EPS)
        return centred * r, r

    now(t_.pre)
    if comm:
        for zz in range(4):
            tot = None
            for w in range(4):
                for q in range(2):
                    b = small[zz, w, q].astype(F32)
                    tot = b if tot is None else tot + b
            vec[0:16, zz * 128 : (zz + 1) * 128] = tot
            for w in range(4):
                two = (small[zz, w, 0].astype(F32) + small[zz, w, 1].astype(F32))[UPB : UPB + 1]
                vec[16 + zz : 17 + zz, w * 128 : (w + 1) * 128] = two
    else:
        vec[0:16] = vec_in[...]
        vec[16:20] = upb_in[...]

    def first_norm(r):
        t = tok(r)
        n, _ = norm(xv[t].astype(F32))
        h = (n * v(LN1G) + v(LN1B)).astype(BF)
        h1[t] = h
        h1t[:, t] = h.T

    rows_loop(first_norm, unroll=2)
    lane = lax.broadcasted_iota(jnp.int32, (slots, 128), 1)
    first_half = lane < HEAD_DIM

    def heads_apart(pair):
        nil = jnp.zeros_like(pair)
        return jnp.where(first_half, pair, nil), jnp.where(first_half, nil, pair)

    for j, (off, w) in enumerate(GROUPS):
        now(t_.proj[j])
        if not comm:
            lc[j].wait()
        shift_ = jnp.concatenate([v(QB)[:, off : off + w], jnp.zeros((1, w), F32), v(VB)[:, off : off + w]], axis=1)
        mult = jnp.where(lax.broadcasted_iota(jnp.int32, (1, 3 * w), 1) < w, SCALE, 1.0)

        def attend(r, j=j, off=off, w=w, shift_=shift_, mult=mult):
            t = tok(r)
            proj = ((nn(h1[t], w_qkv[j][...].reshape(D, 3 * w)) + shift_) * mult).astype(BF)
            qkv[j][t] = proj
            for p in range(w // 128):
                q = proj[:, p * 128 : (p + 1) * 128]
                k = proj[:, w + p * 128 : w + (p + 1) * 128]
                u = proj[:, 2 * w + p * 128 : 2 * w + (p + 1) * 128]
                sc = nt(jnp.concatenate(heads_apart(k), axis=0), q)
                ps = []
                for h in range(2):
                    sh = sc[h * slots : (h + 1) * slots] + bias[r]
                    e = jnp.exp(sh - jnp.max(sh, axis=0, keepdims=True))
                    ps.append((e * (1.0 / jnp.sum(e, axis=0, keepdims=True))).astype(BF))
                probs = jnp.concatenate(ps, axis=0)
                pt[r, off // 128 + p] = probs
                m = tn(probs, jnp.concatenate(heads_apart(u), axis=0))
                mixed[t, pl.ds(off + p * 128, 128)] = m.astype(BF)

        rows_loop(attend, t_.attend[j], unroll=2)
    cg.wait()
    if not comm:
        lc[n_groups].wait()

    def second_norm(r):
        t = tok(r)
        x1 = xv[t].astype(F32) + (nn(mixed[t], w_out[...].reshape(D, D)) + v(OB))
        n, rr = norm(x1)
        h = (n * v(LN2G) + v(LN2B)).astype(BF)
        h2[t] = h
        h2t[:, t] = h.T
        n2[t] = n
        r2[t] = jnp.broadcast_to(rr, (slots, 128))
        x1v[t] = x1
        add(DB, col(gv[t].astype(F32)))

    rows_loop(second_norm, t_.second_norm, unroll=2)
    if not comm:
        lc[n_groups + 1].wait()

    def grads(i, j):
        cut = pl.ds(pl.multiple_of(i * (fc // 2), fc // 2), fc // 2)
        g = tn(act[j * tokens : (j + 1) * tokens, cut], gv[...])
        g_dn[j, pl.ds(2 * i, 2)] = g.astype(BF).reshape(2, *g_dn.shape[2:])
        cut = pl.ds(pl.multiple_of(i * (D // 2), D // 2), D // 2)
        g = nn(h2t[cut], dpre_s[(j % 2) * tokens : (j % 2 + 1) * tokens])
        g_up[j][pl.ds(2 * i, 2)] = g.astype(BF).reshape(2, *g_up[j].shape[1:])

    for j in range(CHUNKS):
        if not comm:
            lc[n_groups + 2 + j].wait()
        ub = vec[16 + j : 17 + j, :]

        def feed(r, j=j, ub=ub):
            t = tok(r)
            wu = w_up[j][...].reshape(D, fc)
            wd = w_dn[j].reshape(fc, D)
            pre = nn(h2[t], wu) + ub
            sq_ = pre * pre
            c1 = 0.5 + 0.5 * jnp.tanh(pre * (GELU_A + GELU_B * sq_))
            a = pre * c1
            slope = c1 + a * ((1.0 - c1) * (2.0 * GELU_A + 6.0 * GELU_B * sq_))
            dpre = nt(gv[t], wd) * slope
            dl = dpre.astype(BF)
            act[pl.ds(pl.multiple_of(j * tokens + r * slots, slots), slots)] = a.astype(BF)
            dpre_s[pl.ds(pl.multiple_of((j % 2) * tokens + r * slots, slots), slots)] = dl
            add(12 + j, col(dpre))
            back = nt(dl, wu)
            dh2[t] = back if j == 0 else dh2[t] + back

        rows_loop(feed, t_.feed[j], unroll=2, also=functools.partial(grads, j=j - 1) if j else None)
        now(t_.fed[j])
    def second_back(r):
        t = tok(r)
        g2 = dh2[t]
        n = n2[t]
        add(LN2G, col(g2 * n))
        add(LN2B, col(g2))
        e = g2 * v(LN2G)
        dx = gv[t].astype(F32) + r2[t, pl.ds(0, 1)] * (
            e - jnp.mean(e, axis=-1, keepdims=True) - n * jnp.mean(e * n, axis=-1, keepdims=True))
        dx1[t] = dx
        add(OB, col(dx))
        da[t] = dx.astype(BF)

    rows_loop(second_back, t_.second_back, unroll=2, also=functools.partial(grads, j=CHUNKS - 1))
    now(t_.after)

    def grad_out(i):
        cut = pl.ds(pl.multiple_of(i * (D // 2), D // 2), D // 2)
        g_wout[pl.ds(2 * i, 2)] = tn(mixed[:, cut], da[...]).astype(BF).reshape(2, *g_wout.shape[1:])


    for j in reversed(range(n_groups)):
        off, w = GROUPS[j]

        def back(r, j=j, off=off, w=w):
            t = tok(r)
            wo_ = w_out[...].reshape(D, D)[off : off + w]
            dmix = nt(da[t], wo_).astype(BF)
            for p in range(w // 128):
                q = qkv[j][t, pl.ds(p * 128, 128)]
                k = qkv[j][t, pl.ds(w + p * 128, 128)]
                u = qkv[j][t, pl.ds(2 * w + p * 128, 128)]
                dm = dmix[:, p * 128 : (p + 1) * 128]
                probs = pt[r, off // 128 + p]
                dm0, dm1 = heads_apart(dm)
                q0, q1 = heads_apart(q)
                dv = nn(probs[:slots], dm0) + nn(probs[slots:], dm1)
                dpt = nt(jnp.concatenate(heads_apart(u), axis=0), dm)
                ds = []
                for h in range(2):
                    pf = probs[h * slots : (h + 1) * slots].astype(F32)
                    d = dpt[h * slots : (h + 1) * slots]
                    ds.append((pf * (d - jnp.sum(pf * d, axis=0, keepdims=True))).astype(BF))
                dk = nn(ds[0], q0) + nn(ds[1], q1)
                dq = tn(jnp.concatenate(ds, axis=0), jnp.concatenate(heads_apart(k), axis=0)) * SCALE
                s0 = off + p * 128
                sg[QB : QB + 1, s0 : s0 + 128] += col(dq)
                sg[VB : VB + 1, s0 : s0 + 128] += col(dv)
                dproj[j][t, pl.ds(p * 128, 128)] = dq.astype(BF)
                dproj[j][t, pl.ds(w + p * 128, 128)] = dk.astype(BF)
                dproj[j][t, pl.ds(2 * w + p * 128, 128)] = dv.astype(BF)

        rows_loop(back, t_.back[j], unroll=2, also=grad_out if j == n_groups - 1 else None)
        now(t_.gqkv[j])
        g_qkv[j][...] = nn(h1t[...], dproj[j][...]).astype(BF).reshape(g_qkv[j].shape)

    def first_back(r):
        t = tok(r)
        g1 = None
        for j, (off, w) in enumerate(GROUPS):
            part = nt(dproj[j][t], w_qkv[j][...].reshape(D, 3 * w))
            g1 = part if g1 is None else g1 + part
        n, rr = norm(xv[t].astype(F32))
        add(LN1G, col(g1 * n))
        add(LN1B, col(g1))
        e = g1 * v(LN1G)
        dx1[t] = dx1[t] + rr * (e - jnp.mean(e, axis=-1, keepdims=True) - n * jnp.mean(e * n, axis=-1, keepdims=True))
        y = x1v[t] + v(DB)
        for j in range(CHUNKS):
            y = y + nn(act[pl.ds(pl.multiple_of(j * tokens + r * slots, slots), slots)], w_dn[j].reshape(fc, D))
        outv[t] = y.astype(BF)

    rows_loop(first_back, t_.first_back, unroll=2)
    ci = start(1, dx1, ig_hbm)
    co = start(0, outv, out_hbm)
    now(t_.tail)
    if comm:
        for i in range(6):
            hand(i)
        for k in range(4):
            room = me.bytes[id(sem_out), k] // (D * 2)
            wait_for((act, (pl.ds(0, room),)), (sem_out, (k,)))
        wait_for((small, (THREE, 0, 0)), (sem_out, (4,)))
        wait_for((small, (ALL, THREE, 0)), (sem_out, (5,)))
        wait_for((small, (ALL, FOUR, 0)), (sem_out, (6,)))
        te.finish()
        tl.finish()
        for cp in given_back:
            cp.wait()
    else:
        sg_o[...] = sg[...]
        out_c = [start(2 + i, b, o) for i, (b, o) in enumerate(zip(g_qkv + [g_wout, g_dn] + g_up, g_out))]
        for cp in out_c:
            cp.wait()
    co.wait()
    ci.wait()


def run_layer(comm, rows, slots, ff, operands):
    tokens = rows * slots
    fc = ff // CHUNKS
    n_groups = len(GROUPS)
    blk = lambda r, c: (4, 4, 2, r, c)
    pieces = [blk(D // 32, 3 * w) for _, w in GROUPS] + [blk(D // 32, D), blk(ff // 32, D)] + [blk(D // 32, fc)] * CHUNKS
    any_ = pl.BlockSpec(memory_space=pl.ANY)
    vm = pl.BlockSpec(memory_space=pltpu.VMEM)
    in_specs = [any_] * (4 + 9 if comm else 4) + [vm] * (0 if comm else 1)
    out_shape = [jax.ShapeDtypeStruct((tokens, D), BF), jax.ShapeDtypeStruct((tokens, D), F32)]
    out_specs = [any_, any_]
    if comm:
        in_specs += [any_] * 4
        out_shape += [jax.ShapeDtypeStruct(s, F32) for s in (
            (D // 32, 3 * D), (D // 32, D), (D // 32, ff), (ff // 32, D), (8, 128), (1, 128))]
        out_specs += [any_] * 6
    else:
        in_specs += [any_] * len(pieces) + [vm]
        out_shape += [jax.ShapeDtypeStruct(s, BF) for s in pieces] + [jax.ShapeDtypeStruct((16, D), F32)]
        out_specs += [any_] * len(pieces) + [vm]
    V = pltpu.VMEM
    scratch = [
        V((tokens, D), BF), V((tokens, D), BF), V((rows, slots, slots), F32), V((tokens, D), BF), V((D, tokens), BF),
        V((rows, D // 128, 2 * slots, slots), BF), V((tokens, D), BF), V((tokens, D), F32), V((tokens, 128), F32),
        V((tokens, D), BF), V((D, tokens), BF), V((tokens, D), F32), V((tokens, D), F32), V((tokens, D), F32),
        V((CHUNKS * tokens, fc), BF), V((2 * tokens, fc), BF), V((tokens, D), BF), V((tokens, D), BF), V((24, D), F32), V((16, D), F32),
        pltpu.SMEM((rows,), jnp.int32), V((rows, slots), jnp.int32),
    ]
    scratch += [V((tokens, 3 * w), BF) for _, w in GROUPS] * 2
    scratch += [V(s, BF) for s in pieces] * 2
    scratch += [pltpu.SemaphoreType.DMA((2 + len(pieces) + 17,))]
    if comm:
        dma = pltpu.SemaphoreType.DMA
        scratch += [V(o.shape, o.dtype) for o in out_shape[2:]] + [V(a.shape, a.dtype) for a in operands[4:13]]
        n_xy = n_groups + 1 + 2 * CHUNKS
        n_z = len(pieces) + 1
        scratch += [V(blk(16, 128), BF), V((14, 32, 128), F32), V((13, 16, 128), F32)]
        scratch += [dma((7,)), dma((n_z,)), dma((n_xy + 1, 3)), dma((n_xy, 3)), dma((n_z,)), dma((4,)), dma((4,))]
        whole = pieces[: n_groups + 1] + pieces[n_groups + 2 :]
        by_way = lambda straight, z, r, c: V((z, r, c) if straight else (2, z, r, c // 2), BF)
        straight = scatter_direct(n_groups)
        for i, s in enumerate(whole):
            r, c = s[3:]
            scratch += [V((4, 4, r, c), BF), by_way(i in straight, 4, r, c), V((2, 4, r, c), BF), V((4, r, c), BF)]
        r, c = pieces[n_groups + 1][3:]
        for j in range(CHUNKS):
            scratch += [V((1, 4, r, c), BF), by_way(len(whole) + j in straight, 1, r, c), V((2, 1, r, c), BF)]
        scratch += [V((4, r, c), BF)]
        scratch += [V((3, *s[3:]), BF) for s in whole] + [V((3, r, c), BF)]
    return pl.pallas_call(
        functools.partial(layer, comm, rows, slots, ff),
        out_shape=out_shape, in_specs=in_specs, out_specs=out_specs, scratch_shapes=scratch,
        compiler_params=pltpu.CompilerParams(
            vmem_limit_bytes=63 << 20, **(dict(collective_id=0, has_side_effects=True) if comm else {})),
        cost_estimate=pl.CostEstimate(flops=22_000_000_000, bytes_accessed=6 << 20, transcendentals=4 << 20),
    )(*operands)


def deliver(n, *refs):
    ins, outs, bufs, sems = refs[: n + 2], refs[n + 2 : n + 2 + n + 9], refs[n + 2 + n + 9 : -1], refs[-1]
    parts = []
    for i in range(n):
        rows = ins[i].shape[0]
        step = min(rows, 256)
        parts += [(i, pl.ds(k, step)) for k in range(0, rows, step)]
    first = [pltpu.make_async_copy(ins[i].at[s], bufs[i].at[s], sems.at[0, k]) for k, (i, s) in enumerate(parts)]
    second = [pltpu.make_async_copy(bufs[i].at[s], outs[i].at[s], sems.at[1, k]) for k, (i, s) in enumerate(parts)]
    for cp in first:
        cp.start()
    for i in range(9):
        o = outs[n + i]
        k = o.shape[0]
        o[...] = (ins[n][i : i + 1, 0:k] if i < 8 else ins[n + 1][:, 0:k]).reshape(k)
    for a, b in zip(first, second):
        a.wait()
        b.start()
    for cp in second:
        cp.wait()


def run_deliver(share, up_share, results):
    n = len(results) - 2
    any_ = pl.BlockSpec(memory_space=pl.ANY)
    vm = pl.BlockSpec(memory_space=pltpu.VMEM)
    n_parts = sum(max(1, r.shape[0] // 256) for r in results[:n])
    return pl.pallas_call(
        functools.partial(deliver, n),
        out_shape=[jax.ShapeDtypeStruct(r.shape, r.dtype) for r in results[:n]]
        + [jax.ShapeDtypeStruct((share,), F32)] * 8 + [jax.ShapeDtypeStruct((up_share,), F32)],
        in_specs=[any_] * n + [vm, vm], out_specs=[any_] * n + [vm] * 9,
        scratch_shapes=[pltpu.VMEM(r.shape, r.dtype) for r in results[:n]] + [pltpu.SemaphoreType.DMA((2, n_parts))],
        compiler_params=pltpu.CompilerParams(vmem_limit_bytes=63 << 20),
    )(*results)


def shards(
    inputs, lengths, slot_order, ln1_gain, ln1_bias, w_qkv, q_bias, v_bias, w_out, out_bias, ln2_gain, ln2_bias, w_up, up_bias,
    w_down, down_bias, cotangent, fast=True,
):
    rows, slots, width = inputs.shape
    tokens = rows * slots
    ff = w_up.shape[1]
    flat = (inputs.reshape(tokens, width), cotangent.reshape(tokens, width), lengths, slot_order)
    vectors = [ln1_gain, ln1_bias, q_bias, v_bias, out_bias, ln2_gain, ln2_bias, down_bias, up_bias]
    axes = ("dp", "shard")
    if fast:
        res = run_layer(True, rows, slots, ff, flat + (*vectors, w_qkv, w_out, w_up, w_down))
        out, ig, gqkv, gout, gup, gdn, *mine, upb = run_deliver(ln1_gain.shape[0], up_bias.shape[0], res)
    else:
        full = lambda a: lax.all_gather(a, axes, axis=0, tiled=True)
        whole = [full(a).astype(F32) for a in vectors]
        packed = jnp.stack(whole[:8] + [jnp.zeros((width,), F32)] * 8)
        wq, wo, wu, wd = full(w_qkv), full(w_out), full(w_up), full(w_down)
        fc = ff // CHUNKS
        cut = lambda a: a.reshape(4, 4, 2, a.shape[0] // 32, a.shape[1])
        pieces = [cut(jnp.concatenate([wq[:, t * D + off : t * D + off + w] for t in range(3)], axis=1)) for off, w in GROUPS]
        pieces += [cut(wo), cut(wd)] + [cut(wu[:, j * fc : (j + 1) * fc]) for j in range(CHUNKS)]
        res = run_layer(False, rows, slots, ff, flat + (packed, *pieces, whole[8].reshape(CHUNKS, fc)))
        out, ig, sg = res[0], res[1], res[-1]
        back = [r.astype(F32).reshape(-1, r.shape[-1]) for r in res[2:-1]]
        own = lambda a: lax.psum_scatter(a, axes, scatter_dimension=0, tiled=True)
        k = len(GROUPS)
        gq = jnp.concatenate([back[j][:, t * w : (t + 1) * w] for t in range(3) for j, (_, w) in enumerate(GROUPS)], axis=1)
        gqkv, gout, gdn, gup = own(gq), own(back[k]), own(back[k + 1]), own(jnp.concatenate(back[k + 2 :], axis=1))
        mine = own(sg[0:8].T).T
        upb = own(sg[12:16].reshape(-1))
    shape = (rows, slots, width)
    return (
        out.reshape(shape), ig.reshape(shape), mine[LN1G], mine[LN1B], gqkv, mine[QB], mine[VB], gout, mine[OB], mine[LN2G],
        mine[LN2B], gup, upb, gdn, mine[DB],
    )


def solution(mesh):
    whole = P(("dp", "shard"))
    fast = mesh.shape["dp"] == 8 and mesh.shape["shard"] == 4
    return jax.shard_map(
        functools.partial(shards, fast=fast), mesh=mesh, in_specs=(whole,) * 17, out_specs=(whole,) * 15, check_vma=False)
```
